256 devices in a mesh: gx: 8 (over z_lo, core), gy: 32 (over z_hi, y, x).
Axes of the slice: x: 4, y: 4, z: 8 (z_hi: 2, z_lo: 4; z = z_hi * 4 + z_lo), core: 2. Of those that a mesh axis runs over, the one named last changes fastest.
Arguments:
- features: bfloat16 [8, 512, 64, 128], P('gx', 'gy'), may hold values from -6 to 6
- block_at: int32 [64, 256, 16], P('gx', 'gy'), may hold values from -1 to 15, as said below
- block_coords: int32 [8, 3, 512], P('gx', None, 'gy'), may hold values from 0 to 15, as said below
- weight: bfloat16 [3456, 128], P('gy'), may hold values from -0.109375 to 0.109375
- cotangent: bfloat16 [8, 512, 64, 128], P('gx', 'gy'), may hold values from -6 to 6
Outputs:
- output: bfloat16 [8, 512, 64, 128], P('gx', 'gy')
- grad_features: bfloat16 [8, 512, 64, 128], P('gx', 'gy')
- grad_weight: float32 [3456, 128], P('gy')
The draws below stay inside these ranges and needn't reach their ends.
Inputs may be any that keep to these rules, and one draw needn't show every extreme that they name: `block_at`: each entry is the slot, among the 16 slots of the device owning that position, of the active block placed there, or -1 for an empty position. A slot appears at most once in a tile; every tile has between 8 and 16 active slots, and some tile has all 16 active. `block_coords`: for each slot, its block position (first, second, third coordinate) within its device's 8 x 8 x 16 tile; the positions of one tile's slots are distinct, and a slot is active exactly when block_at at its position holds it (otherwise the position is empty).
All inputs are finite; a program needn't handle non-finite values.
Results may differ from the reference program's by a relative error of at most 0.001.
Values may be sent and summed in bfloat16 or wider, within the bound.
A program may use at most 128 MiB of HBM per device.

```python
import math
import jax
import jax.numpy as jnp
from jax import lax

C = 128
NB = 16
TBX = 8
TBY = 8
TBZ = 16
SLOTS = 512
N_GX = 8
N_GY = 32


def tile_layout(key):
    tiles = N_GX * N_GY
    positions = TBX * TBY * TBZ
    tile_keys = jax.random.split(jax.random.fold_in(key, 101), tiles)
    chosen = jax.vmap(lambda single: jax.random.permutation(single, positions))(tile_keys)[:, :NB].astype(jnp.int32)
    live_count = jax.random.randint(jax.random.fold_in(key, 102), (tiles,), NB // 2, NB + 1)
    full_tile = jax.random.randint(jax.random.fold_in(key, 103), (), 0, tiles)
    live_count = jnp.where(jnp.arange(tiles) == full_tile, NB, live_count)
    slot_ids = jnp.arange(NB, dtype=jnp.int32)
    values = jnp.where(slot_ids[None, :] < live_count[:, None], slot_ids[None, :], -1).astype(jnp.int32)
    grids = jnp.full((tiles, positions), -1, jnp.int32)
    grids = grids.at[jnp.arange(tiles)[:, None], chosen].set(values)
    return (chosen, grids)


def draw_block_at(key, part):
    chosen, grids = tile_layout(key)
    grids = grids.reshape(N_GX, N_GY, TBX, TBY, TBZ).transpose(0, 2, 1, 3, 4)
    return grids.reshape(N_GX * TBX, N_GY * TBY, TBZ)


def draw_block_coords(key, part):
    chosen, grids = tile_layout(key)
    coord_x = chosen // (TBY * TBZ)
    coord_y = chosen // TBZ % TBY
    coord_z = chosen % TBZ
    stacked = jnp.stack([coord_x, coord_y, coord_z], axis=0).astype(jnp.int32)
    return stacked.reshape(3, N_GX, N_GY, NB).transpose(1, 0, 2, 3).reshape(N_GX, 3, N_GY * NB)


def block_scale(rng, extent, cuts, smallest, top_value):
    def one(axis_at, blocks):
        heights = jax.random.uniform(jax.random.fold_in(jax.random.fold_in(rng, 6), axis_at), (blocks,), jnp.float32, smallest / len(cuts), top_value / len(cuts))
        return jnp.repeat(jnp.exp(heights), extent[axis_at] // blocks).reshape((-1,) + (1,) * (len(extent) - axis_at - 1))

    factor_of = one(*cuts[0])
    for cut in cuts[1:]:
        factor_of = factor_of * one(*cut)
    return factor_of


def noise(own_key, extent, width, bound, pieces=(), kind=jnp.bfloat16):
    drawn = width * jax.random.normal(own_key, extent, jnp.float32)
    if pieces:
        drawn = drawn * block_scale(own_key, extent, pieces, -0.22, 0.18)
    return jnp.clip(drawn, -bound, bound).astype(kind)


def setup_inputs(seed: int = 0) -> dict:
    key_of = jax.random.split(jax.random.key(seed), 6)
    return {
        "features": noise(key_of[0], (N_GX, SLOTS, 64, C), 1.0, 6.0, ((0, 8), (1, 32))),
        "block_at": draw_block_at(jax.random.fold_in(key_of[5], 71), 0),
        "block_coords": draw_block_coords(jax.random.fold_in(key_of[5], 71), 0),
        "weight": noise(key_of[3], (27 * C, C), (27 * C) ** -0.5, 0.109375, ((0, 32),)),
        "cotangent": noise(key_of[4], (N_GX, SLOTS, 64, C), 1.0, 6.0, ((0, 8), (1, 32))),
    }


def assemble(pool, neighbours):
    ranges = ((3, 4), (0, 4), (0, 1))
    slab_list = []
    for along_x in range(3):
        row_list = []
        for along_y in range(3):
            cell_list = []
            for along_z in range(3):
                blocks_taken = jnp.take(pool, neighbours[:, (along_x * 3 + along_y) * 3 + along_z], axis=0)
                cell_list.append(blocks_taken[:, ranges[along_x][0]:ranges[along_x][1], ranges[along_y][0]:ranges[along_y][1], ranges[along_z][0]:ranges[along_z][1], :])
            row_list.append(jnp.concatenate(cell_list, axis=3))
        slab_list.append(jnp.concatenate(row_list, axis=2))
    return jnp.concatenate(slab_list, axis=1)

def unfold(padded):
    block_count = padded.shape[0]
    channels = padded.shape[-1]
    windows = []
    for along_x in range(3):
        for along_y in range(3):
            for along_z in range(3):
                windows.append(padded[:, along_x:along_x + 4, along_y:along_y + 4, along_z:along_z + 4, :].reshape(block_count * 64, channels))
    return jnp.concatenate(windows, axis=1)

def reference(features, block_at, block_coords, weight, cotangent):
    tiles = N_GX * N_GY
    total_slots = tiles * NB

    def as_pool(field):
        blocks = field.reshape(total_slots, 4, 4, 4, C)
        return jnp.concatenate([blocks, jnp.zeros((1, 4, 4, 4, C), field.dtype)], axis=0)
    tile_x = (jnp.arange(N_GX * TBX, dtype=jnp.int32) // TBX)[:, None, None]
    tile_y = (jnp.arange(N_GY * TBY, dtype=jnp.int32) // TBY)[None, :, None]
    global_id = jnp.where(block_at >= 0, (tile_x * N_GY + tile_y) * NB + block_at, total_slots).astype(jnp.int32)
    padded_id = jnp.pad(global_id, 1, constant_values=total_slots).reshape(-1)
    coords = block_coords.reshape(N_GX, 3, N_GY, NB).transpose(0, 2, 1, 3).reshape(tiles, 3, NB)
    tile_index = jnp.arange(tiles, dtype=jnp.int32)
    anchor_x = tile_index // N_GY * TBX
    anchor_y = tile_index % N_GY * TBY
    stride_x = (N_GY * TBY + 2) * (TBZ + 2)
    stride_y = TBZ + 2
    offset_list = []
    for along_x in range(3):
        for along_y in range(3):
            for along_z in range(3):
                offset_list.append(along_x * stride_x + along_y * stride_y + along_z)
    offset_table = jnp.array(offset_list, dtype=jnp.int32)
    position = (coords[:, 0] + anchor_x[:, None]) * stride_x + (coords[:, 1] + anchor_y[:, None]) * stride_y + coords[:, 2]
    flat = position[:, :, None] + offset_table[None, None, :]
    neighbours = jnp.take(padded_id, flat, axis=0).astype(jnp.int32)
    live = neighbours[:, :, 13] == tile_index[:, None] * NB + jnp.arange(NB, dtype=jnp.int32)[None, :]
    flipped = weight.reshape(27, C, C)[::-1].transpose(0, 2, 1).reshape(27 * C, C)
    pool_u = as_pool(features)
    pool_g = as_pool(cotangent)
    cot_rows = cotangent.reshape(tiles, NB * 64, C)

    def per_tile(total, inputs):
        near, alive, grad_rows = inputs
        cell_live = jnp.repeat(alive, 64)[:, None]
        cols_u = unfold(assemble(pool_u, near))
        forward = jnp.dot(cols_u, weight, preferred_element_type=jnp.float32)
        forward = jnp.where(cell_live, forward, 0.0).astype(jnp.bfloat16)
        cols_g = unfold(assemble(pool_g, near))
        backward = jnp.dot(cols_g, flipped, preferred_element_type=jnp.float32)
        backward = jnp.where(cell_live, backward, 0.0).astype(jnp.bfloat16)
        kept_grad = jnp.where(cell_live, grad_rows, jnp.zeros_like(grad_rows))
        total = total + jnp.dot(cols_u.T, kept_grad, preferred_element_type=jnp.float32)
        return (total, (forward, backward))
    grad_total, (outs, grads) = lax.scan(per_tile, jnp.zeros((27 * C, C), jnp.float32), (neighbours, live, cot_rows))
    grad_weight = grad_total * (1.0 / math.sqrt(N_GX * N_GY * NB * 64))
    return (outs.reshape(N_GX, N_GY * NB, 64, C), grads.reshape(N_GX, N_GY * NB, 64, C), grad_weight)
```

```python
import functools
import math

import jax
import jax.numpy as jnp
from jax import lax
from jax.experimental import pallas as pl
from jax.experimental.pallas import tpu as pltpu
from jax.sharding import PartitionSpec as P

MESH = pl.DeviceIdType.MESH
F32 = jnp.float32
BF16 = jnp.bfloat16
CH = 128
NB = 16
TAPS = 27
NOWHERE = -1.0e6


def iota(shape, dim):
    return lax.broadcasted_iota(jnp.int32, shape, dim)


def zero_one(mask):
    return jnp.where(mask, 1.0, 0.0).astype(BF16)


def exact_dot(left, right):
    return jnp.dot(left, right, preferred_element_type=F32)


def kernel(
    gx_size,
    gy_size,
    f_ref,
    at_ref,
    coords_ref,
    w_ref,
    g_ref,
    out_ref,
    gf_ref,
    gw_ref,
    send,
    field,
    halo_x,
    halo_y,
    halo_d,
    w_pair,
    w_parts,
    w_full,
    dw_full,
    dw_parts,
    swap_in,
    chip_sum,
    plane_in,
    plane_sum,
    z_in,
    final,
    halo_send,
    halo_recv,
    wz_send,
    wz_recv,
    wp_send,
    wp_recv,
    ws_send,
    ws_recv,
    r0_send,
    r0_recv,
    r1_send,
    r1_recv,
    r2_send,
    r2_recv,
    r3_send,
    r3_recv,
):
    plane = gy_size // 2
    z_low = gx_size // 2
    z_all = 2 * z_low
    rows = TAPS * CH // gy_size
    half = rows // 2
    half_pad = final.shape[1]
    p = lax.axis_index("gx")
    q = lax.axis_index("gy")
    core = lax.rem(p, 2)
    zlo = p // 2
    zhi = q // plane
    spot = lax.rem(q, plane)
    zed = zhi * z_low + zlo

    sibling = (p + 1 - 2 * core, q)
    partner = (p, spot + (1 - zhi) * plane)
    plane_peers = [(p, zhi * plane + lax.rem(spot + k, plane)) for k in range(1, plane)]
    z_peers = []
    for k in range(1, z_all):
        other = lax.rem(zed + k, z_all)
        z_peers.append((lax.rem(other, z_low) * 2 + core, (other // z_low) * plane + spot))
    around = []
    for dx in (-1, 0, 1):
        for dy in (-1, 0, 1):
            if dx or dy:
                around.append((dx, dy))

    def at(dx, dy):
        return (lax.rem(p + dx + gx_size, gx_size), lax.rem(q + dy + gy_size, gy_size))

    barrier = pltpu.get_barrier_semaphore()
    greeted = [sibling, partner] + plane_peers + z_peers + [at(dx, dy) for dx, dy in around]
    for device in greeted:
        pl.semaphore_signal(barrier, inc=1, device_id=device, device_id_type=MESH)

    lane_slot = lax.rem(iota((1, CH), 1), NB).astype(F32)
    found = jnp.zeros((at_ref.shape[0], CH), F32)
    placed = at_ref[...].astype(F32)
    for z in range(placed.shape[1]):
        found = jnp.maximum(found, jnp.where(placed[:, z : z + 1] == lane_slot, 1.0, 0.0))
    live = jnp.max(found, axis=0, keepdims=True)
    spread = zero_one(lax.rem(iota((NB, CH), 1), NB) == iota((NB, CH), 0))
    coords = coords_ref[0].astype(F32).astype(BF16)
    place = exact_dot(coords, spread)
    lined = jnp.concatenate([place, live, jnp.zeros((NB - 4, CH), F32)], axis=0)
    meta = jnp.concatenate([lined, lined], axis=1).astype(BF16)

    live_rows = jnp.broadcast_to(live[:, :NB], (8, NB)).astype(BF16)
    by_high = zero_one(iota((NB, NB * NB), 1) // NB == iota((NB, NB * NB), 0))
    by_low = zero_one(lax.rem(iota((NB, NB * NB), 1), NB) == iota((NB, NB * NB), 0))
    live_high = exact_dot(live_rows, by_high)[0:1]
    live_low = exact_dot(live_rows, by_low)[0:1]
    row_id = iota((NB * NB, NB * NB), 0)
    col_id = iota((NB * NB, NB * NB), 1)
    turned = (lax.rem(row_id, NB) == col_id // NB) & (row_id // NB == lax.rem(col_id, NB))
    turn = jnp.where(turned, 1.0, 0.0)
    turn_in = (turn * live_high).astype(BF16)
    turn_out = (turn * live_low).astype(BF16)
    for i in range(4):
        cells = pl.ds(16 * i, 16)
        both = jnp.concatenate(
            [f_ref[0, :, cells, :].reshape(256, CH), g_ref[0, :, cells, :].reshape(256, CH)], axis=1
        )
        slab = exact_dot(turn_in, both).astype(BF16).reshape(4, 4, NB, 2 * CH)
        send[i, :, 0:4] = slab
        field[i + 1, 1:5, 1:5] = slab
        for j in range(4):
            send[i, j, 4] = meta

    pad_rows = w_pair.shape[1]
    w_pair[zhi] = jnp.zeros((pad_rows, CH), BF16)
    w_pair[zhi, 0:rows] = w_ref[...]
    pl.semaphore_wait(barrier, len(greeted))

    def push(src, dst, send_sem, recv_sem, device):
        copy = pltpu.make_async_remote_copy(
            src_ref=src,
            dst_ref=dst,
            send_sem=send_sem,
            recv_sem=recv_sem,
            device_id=device,
            device_id_type=MESH,
        )
        copy.start()
        return copy

    halo_copies = []
    for index, (dx, dy) in enumerate(around):
        face_x = 3 if dx > 0 else 0
        face_y = 3 if dy > 0 else 0
        to_x = 0 if dx > 0 else 1
        to_y = 0 if dy > 0 else 1
        if dy == 0:
            src, dst = send.at[face_x], halo_x.at[to_x]
        elif dx == 0:
            src, dst = send.at[:, face_y], halo_y.at[to_y]
        else:
            src, dst = send.at[face_x, face_y], halo_d.at[to_x, to_y]
        halo_copies.append(
            push(src, dst, halo_send.at[index], halo_recv.at[index], at(dx, dy))
        )
    wz_copy = push(w_pair.at[zhi], w_pair.at[zhi], wz_send.at[0], wz_recv.at[0], partner)
    wz_copy.wait()
    wp_copies = []
    mine = core * plane + spot
    w_parts[mine] = w_pair[core]
    for k, device in enumerate(plane_peers):
        wp_copies.append(
            push(w_pair.at[core], w_parts.at[mine], wp_send.at[k], wp_recv.at[k], device)
        )
    for copy in halo_copies:
        copy.wait()

    def code_of(tile, dx, dy):
        values = tile[...].astype(F32)
        code = (values[0:1] + 8.0 * dx) * 1024.0 + (values[1:2] + 8.0 * dy) * 32.0 + values[2:3]
        there = values[3:4] > 0.5
        if dx:
            inside = (p + dx >= 0) & (p + dx < gx_size)
            there = there & inside
        if dy:
            inside = (q + dy >= 0) & (q + dy < gy_size)
            there = there & inside
        return jnp.where(there, code, NOWHERE)

    codes = {(0, 0): code_of(send.at[0, 0, 4, :, 0:CH], 0, 0)}
    for dx, dy in around:
        low_x = 0 if dx < 0 else 1
        low_y = 0 if dy < 0 else 1
        if dy == 0:
            tile = halo_x.at[low_x, 0, 4, :, 0:CH]
        elif dx == 0:
            tile = halo_y.at[low_y, 0, 4, :, 0:CH]
        else:
            tile = halo_d.at[low_x, low_y, 4, :, 0:CH]
        codes[(dx, dy)] = code_of(tile, dx, dy)
    own_place = (place[0:1] * 1024.0 + place[1:2] * 32.0 + place[2:3])[:, :NB]
    diagonal = iota((NB, NB), 0) == iota((NB, NB), 1)
    own_code = jnp.sum(jnp.where(diagonal, own_place, 0.0), axis=1, keepdims=True)

    def source(dx, dy, i, j, k):
        if dx == 0 and dy == 0:
            return send[i, j, k]
        low_x = 0 if dx < 0 else 1
        low_y = 0 if dy < 0 else 1
        if dy == 0:
            return halo_x[low_x, j, k]
        if dx == 0:
            return halo_y[low_y, i, k]
        return halo_d[low_x, low_y, k]

    def padded(cell, shift):
        return 0 if shift < 0 else (5 if shift > 0 else cell + 1)

    for along_x in (-1, 0, 1):
        for along_y in (-1, 0, 1):
            xs = (0, along_x) if along_x else (0,)
            ys = (0, along_y) if along_y else (0,)
            tiles = [(dx, dy) for dx in xs for dy in ys]
            depth = NB * len(tiles)
            group = iota((1, depth), 1) // NB
            code_row = codes[tiles[0]][:, :depth]
            for n in range(1, len(tiles)):
                code_row = jnp.where(group == n, codes[tiles[n]][:, :depth], code_row)
            pieces = []
            for oz in (-1, 0, 1):
                for ox, oy in tiles:
                    wanted = own_code + float(ox * 1024 + oy * 32 + oz)
                    pieces.append(jnp.where(wanted == code_row, 1.0, 0.0))
            picks = jnp.concatenate(pieces, axis=0).astype(BF16)
            count = len(tiles)
            x_list = (3,) if along_x < 0 else ((0,) if along_x > 0 else (1, 2))
            y_list = (3,) if along_y < 0 else ((0,) if along_y > 0 else (1, 2))
            for i in x_list:
                for j in y_list:
                    for k in range(4):
                        shifts = (-1, 0) if k == 3 else ((0, 1) if k == 0 else (0,))
                        if count == 1 and k in (1, 2):
                            continue
                        first = (shifts[0] + 1) * count * NB
                        last = (shifts[-1] + 2) * count * NB
                        pool = [source(dx, dy, i, j, k) for dx, dy in tiles]
                        pool = pool[0] if count == 1 else jnp.concatenate(pool, axis=0)
                        got = exact_dot(picks[first:last], pool).astype(BF16)
                        at_row = 0
                        for oz in shifts:
                            for ox, oy in tiles:
                                if ox or oy or oz:
                                    field[padded(i, ox), padded(j, oy), padded(k, oz)] = got[
                                        at_row : at_row + NB
                                    ]
                                at_row += NB

    def window(tap, low):
        a, b, e = tap // 9, tap // 3 % 3, tap % 3
        return field[a : a + 4, b : b + 4, e : e + 4, :, low : low + CH].reshape(1024, CH)

    kept = field[1:5, 1:5, 1:5, :, CH : 2 * CH].reshape(1024, CH)
    dw_full[TAPS * CH :] = jnp.zeros((dw_full.shape[0] - TAPS * CH, CH), F32)
    for tap in range(TAPS):
        dw_full[tap * CH : (tap + 1) * CH] = lax.dot_general(
            window(tap, 0), kept, (((0,), (0,)), ((), ())), preferred_element_type=F32
        )
    for index in range(gy_size):
        for part in range(2):
            start = index * rows + part * half
            dw_parts[part, index % plane, index // plane] = dw_full[start : start + half_pad]
    swap_copy = push(dw_parts.at[1 - core], swap_in, r0_send.at[0], r0_recv.at[0], sibling)

    for copy in wp_copies:
        copy.wait()
    ours = w_parts.at[pl.ds(core * plane, plane)]
    ws_copy = push(ours, ours, ws_send.at[0], ws_recv.at[0], sibling)

    swap_copy.wait()
    chip_sum[...] = dw_parts[core] + swap_in[...]
    plane_copies = []
    for k, device in enumerate(plane_peers):
        plane_copies.append(
            push(
                chip_sum.at[lax.rem(spot + k + 1, plane)],
                plane_in.at[k],
                r1_send.at[k],
                r1_recv.at[k],
                device,
            )
        )

    ws_copy.wait()
    for index in range(gy_size):
        w_full[index * rows : (index + 1) * rows] = w_parts[index, 0:rows]

    forward = jnp.zeros((1024, CH), F32)
    for tap in range(0, TAPS, 2):
        last = min(tap + 2, TAPS)
        left = [window(n, 0) for n in range(tap, last)]
        left = left[0] if len(left) == 1 else jnp.concatenate(left, axis=1)
        forward = forward + exact_dot(left, w_full[tap * CH : last * CH])
    forward = forward.astype(BF16)
    for i in range(4):
        slab = exact_dot(turn_out, forward[256 * i : 256 * i + 256]).astype(BF16)
        out_ref[0, :, 16 * i : 16 * i + 16, :] = slab.reshape(NB, 16, CH)

    for copy in plane_copies:
        copy.wait()
    total = chip_sum[spot]
    for k in range(plane - 1):
        total = total + plane_in[k]
    plane_sum[...] = total
    z_copies = []
    for k, device in enumerate(z_peers):
        other = lax.rem(zed + k + 1, z_all) // z_low
        z_copies.append(
            push(plane_sum.at[other], z_in.at[k], r2_send.at[k], r2_recv.at[k], device)
        )

    backward = jnp.zeros((1024, CH), F32)
    for tap in range(0, TAPS, 2):
        last = min(tap + 2, TAPS)
        left = [window(26 - n, CH) for n in range(tap, last)]
        right = [w_full[n * CH : (n + 1) * CH] for n in range(tap, last)]
        left = left[0] if len(left) == 1 else jnp.concatenate(left, axis=1)
        right = right[0] if len(right) == 1 else jnp.concatenate(right, axis=1)
        backward = backward + lax.dot_general(
            left, right, (((1,), (1,)), ((), ())), preferred_element_type=F32
        )
    backward = backward.astype(BF16)
    for i in range(4):
        slab = exact_dot(turn_out, backward[256 * i : 256 * i + 256]).astype(BF16)
        gf_ref[0, :, 16 * i : 16 * i + 16, :] = slab.reshape(NB, 16, CH)

    for copy in z_copies:
        copy.wait()
    total = plane_sum[zhi]
    for k in range(z_all - 1):
        total = total + z_in[k]
    final[core] = total * (1.0 / math.sqrt(gx_size * gy_size * NB * 64))
    last_copy = push(final.at[core], final.at[core], r3_send.at[0], r3_recv.at[0], sibling)
    last_copy.wait()
    for part in range(2):
        gw_ref[part * half : (part + 1) * half] = final[part, 0:half]


def local(gx_size, gy_size, features, block_at, block_coords, weight, cotangent):
    plane = gy_size // 2
    z_all = gx_size
    rows = TAPS * CH // gy_size
    rows_pad = -(-rows // 16) * 16
    half_pad = -(-(rows // 2) // 8) * 8
    blocks = pl.BlockSpec(memory_space=pltpu.VMEM)
    dma = pltpu.SemaphoreType.DMA
    return pl.pallas_call(
        functools.partial(kernel, gx_size, gy_size),
        out_shape=(
            jax.ShapeDtypeStruct(features.shape, BF16),
            jax.ShapeDtypeStruct(features.shape, BF16),
            jax.ShapeDtypeStruct((rows, CH), F32),
        ),
        in_specs=[blocks] * 5,
        out_specs=[blocks] * 3,
        scratch_shapes=[
            pltpu.VMEM((4, 4, 5, NB, 2 * CH), BF16),
            pltpu.VMEM((6, 6, 6, NB, 2 * CH), BF16),
            pltpu.VMEM((2, 4, 5, NB, 2 * CH), BF16),
            pltpu.VMEM((2, 4, 5, NB, 2 * CH), BF16),
            pltpu.VMEM((2, 2, 5, NB, 2 * CH), BF16),
            pltpu.VMEM((2, rows_pad, CH), BF16),
            pltpu.VMEM((gy_size, rows_pad, CH), BF16),
            pltpu.VMEM((TAPS * CH, CH), BF16),
            pltpu.VMEM((TAPS * CH + 16, CH), F32),
            pltpu.VMEM((2, plane, 2, half_pad, CH), F32),
            pltpu.VMEM((plane, 2, half_pad, CH), F32),
            pltpu.VMEM((plane, 2, half_pad, CH), F32),
            pltpu.VMEM((plane - 1, 2, half_pad, CH), F32),
            pltpu.VMEM((2, half_pad, CH), F32),
            pltpu.VMEM((z_all - 1, half_pad, CH), F32),
            pltpu.VMEM((2, half_pad, CH), F32),
            dma((8,)),
            dma((8,)),
            dma((1,)),
            dma((1,)),
            dma((plane - 1,)),
            dma((plane - 1,)),
            dma((1,)),
            dma((1,)),
            dma((1,)),
            dma((1,)),
            dma((plane - 1,)),
            dma((plane - 1,)),
            dma((z_all - 1,)),
            dma((z_all - 1,)),
            dma((1,)),
            dma((1,)),
        ],
        compiler_params=pltpu.CompilerParams(
            collective_id=0, has_side_effects=True, vmem_limit_bytes=48 * 1024 * 1024
        ),
    )(features, block_at.reshape(-1, block_at.shape[2]), block_coords, weight, cotangent)


def solution(mesh):
    placed = (
        P("gx", "gy", None, None),
        P("gx", "gy", None),
        P("gx", None, "gy"),
        P("gy", None),
        P("gx", "gy", None, None),
    )
    return jax.shard_map(
        functools.partial(local, mesh.shape["gx"], mesh.shape["gy"]),
        mesh=mesh,
        in_specs=placed,
        out_specs=(P("gx", "gy", None, None), P("gx", "gy", None, None), P("gy", None)),
        check_vma=False,
    )
```

```python
import functools
import math

import jax
import jax.numpy as jnp
from jax import lax
from jax.experimental import pallas as pl
from jax.experimental.pallas import tpu as pltpu
from jax.sharding import PartitionSpec as P

MESH = pl.DeviceIdType.MESH
F32 = jnp.float32
BF16 = jnp.bfloat16
CH = 128
NB = 16
TAPS = 27
NOWHERE = -1.0e6
AROUND = [(dx, dy) for dx in (-1, 0, 1) for dy in (-1, 0, 1) if dx or dy]


def iota(shape, dim):
    return lax.broadcasted_iota(jnp.int32, shape, dim)


def zero_one(mask):
    return jnp.where(mask, 1.0, 0.0).astype(BF16)


def exact_dot(left, right):
    return jnp.dot(left, right, preferred_element_type=F32)


def face_slot(dx, dy):
    if dy == 0:
        return True, 0 if dx > 0 else 1
    if dx == 0:
        return True, 2 if dy > 0 else 3
    return False, (0 if dx > 0 else 2) + (0 if dy > 0 else 1)


def kernel(
    gx_size,
    gy_size,
    side,
    f_hbm,
    at_hbm,
    coords_hbm,
    w_hbm,
    g_hbm,
    out_ref,
    gf_ref,
    gw_ref,
    f_ref,
    at_ref,
    coords_ref,
    w_ref,
    g_ref,
    field_u,
    field_g,
    send_face,
    send_diag,
    halo_face,
    halo_diag,
    send_gface,
    send_gdiag,
    halo_gface,
    halo_gdiag,
    w_pair,
    w_parts,
    w_full,
    w_turned,
    dw_full,
    dw_parts,
    swap_in,
    chip_sum,
    one_in,
    one_sum,
    two_in,
    plane_sum,
    z_in,
    pieces,
    in_sem,
    hu_send,
    hu_recv,
    hg_send,
    hg_recv,
    wz_sem,
    w1_send,
    w1_recv,
    w2_send,
    w2_recv,
    ws_sem,
    r0_send,
    r0_recv,
    r1_send,
    r1_recv,
    r2_send,
    r2_recv,
    r3_send,
    r3_recv,
    r4_send,
    r4_recv,
):
    plane = side * side
    z_low = gx_size // 2
    z_all = 2 * z_low
    rows = TAPS * CH // gy_size
    half = rows // 2
    half_pad = plane_sum.shape[1]
    piece = pieces.shape[1]
    p = lax.axis_index("gx")
    q = lax.axis_index("gy")
    core = lax.rem(p, 2)
    zlo = p // 2
    zhi = q // plane
    spot = lax.rem(q, plane)
    zed = zhi * z_low + zlo
    x = lax.rem(spot, side)
    y = spot // side
    pos1 = x + core * (y - x)
    pos2 = y + core * (x - y)
    step1 = 1 + core * (side - 1)
    step2 = side - core * (side - 1)

    sibling = (p + 1 - 2 * core, q)
    partner = (p, spot + (1 - zhi) * plane)
    ones = [lax.rem(pos1 + k, side) for k in range(1, side)]
    twos = [lax.rem(pos2 + k, side) for k in range(1, side)]
    peers1 = [(p, zhi * plane + n * step1 + pos2 * step2) for n in ones]
    peers2 = [(p, zhi * plane + pos1 * step1 + n * step2) for n in twos]
    zeds = [lax.rem(zed + k, z_all) for k in range(1, z_all)]
    z_peers = [(lax.rem(z, z_low) * 2 + core, (z // z_low) * plane + spot) for z in zeds]
    gx_peers = [(lax.rem(p + k, gx_size), q) for k in range(1, gx_size)]

    def at(dx, dy):
        return (lax.rem(p + dx + gx_size, gx_size), lax.rem(q + dy + gy_size, gy_size))

    def inside(dx, dy):
        return (p + dx >= 0) & (p + dx < gx_size) & (q + dy >= 0) & (q + dy < gy_size)

    barrier = pltpu.get_barrier_semaphore()
    greeted = [sibling, partner] + peers1 + peers2 + z_peers + gx_peers
    greeted = greeted + [at(dx, dy) for dx, dy in AROUND]
    for device in greeted:
        pl.semaphore_signal(barrier, inc=1, device_id=device, device_id_type=MESH)
    loads = []
    pairs = ((at_hbm, at_ref), (coords_hbm, coords_ref), (f_hbm, f_ref), (g_hbm, g_ref), (w_hbm, w_ref))
    for index, (src, dst) in enumerate(pairs):
        copy = pltpu.make_async_copy(src, dst, in_sem.at[index])
        copy.start()
        loads.append(copy)

    loads[0].wait()
    loads[1].wait()
    lane_slot = lax.rem(iota((1, CH), 1), NB).astype(F32)
    found = jnp.zeros((at_ref.shape[0], CH), F32)
    placed = at_ref[...].astype(F32)
    for z in range(placed.shape[1]):
        found = jnp.maximum(found, jnp.where(placed[:, z : z + 1] == lane_slot, 1.0, 0.0))
    live = jnp.max(found, axis=0, keepdims=True)
    spread = zero_one(lax.rem(iota((NB, CH), 1), NB) == iota((NB, CH), 0))
    coords = coords_ref[0].astype(F32).astype(BF16)
    place = exact_dot(coords, spread)
    meta = jnp.concatenate([place, live, jnp.zeros((NB - 4, CH), F32)], axis=0).astype(BF16)

    live_rows = jnp.broadcast_to(live[:, :NB], (8, NB)).astype(BF16)
    by_high = zero_one(iota((NB, NB * NB), 1) // NB == iota((NB, NB * NB), 0))
    by_low = zero_one(lax.rem(iota((NB, NB * NB), 1), NB) == iota((NB, NB * NB), 0))
    live_high = exact_dot(live_rows, by_high)[0:1]
    live_low = exact_dot(live_rows, by_low)[0:1]
    row_id = iota((NB * NB, NB * NB), 0)
    col_id = iota((NB * NB, NB * NB), 1)
    turned = (lax.rem(row_id, NB) == col_id // NB) & (row_id // NB == lax.rem(col_id, NB))
    turn = jnp.where(turned, 1.0, 0.0)
    turn_in = (turn * live_high).astype(BF16)
    turn_out = (turn * live_low).astype(BF16)

    def take_in(ref, field, faces, diags):
        for i in range(4):
            block = ref[0, :, 16 * i : 16 * i + 16, :].reshape(NB * NB, CH)
            slab = exact_dot(turn_in, block).astype(BF16).reshape(4, 4, NB, CH)
            field[i + 1, 1:5, 1:5] = slab
            for which, along in ((0, 3), (1, 0)):
                if i == along:
                    faces[which, 0:16] = slab.reshape(16, NB, CH)
                    diags[2 * which, 0:4] = slab[3]
                    diags[2 * which + 1, 0:4] = slab[0]
            faces[2, 4 * i : 4 * i + 4] = slab[3]
            faces[3, 4 * i : 4 * i + 4] = slab[0]

    loads[2].wait()
    take_in(f_ref, field_u, send_face, send_diag)
    for n in range(4):
        send_face[n, 16] = meta
        send_diag[n, 4] = meta
    loads[4].wait()
    w_pair[zhi] = jnp.zeros((w_pair.shape[1], CH), BF16)
    w_pair[zhi, 0:rows] = w_ref[...]

    def remote(src, dst, send_sem, recv_sem, device):
        return pltpu.make_async_remote_copy(
            src_ref=src,
            dst_ref=dst,
            send_sem=send_sem,
            recv_sem=recv_sem,
            device_id=device,
            device_id_type=MESH,
        )

    def push(src, dst, send_sem, recv_sem, device):
        copy = remote(src, dst, send_sem, recv_sem, device)
        copy.start()
        return copy

    def halo_copy(index, faces, diags, faces_in, diags_in, send_sem, recv_sem):
        dx, dy = AROUND[index]
        is_face, slot = face_slot(dx, dy)
        src = faces.at[slot] if is_face else diags.at[slot]
        dst = faces_in.at[slot] if is_face else diags_in.at[slot]
        return remote(src, dst, send_sem.at[index], recv_sem.at[index], at(dx, dy))

    def halo_start(*refs):
        for index, (dx, dy) in enumerate(AROUND):

            @pl.when(inside(dx, dy))
            def _():
                halo_copy(index, *refs).start()

    def halo_wait(*refs):
        for index, (dx, dy) in enumerate(AROUND):
            is_face, slot = face_slot(dx, dy)
            landed = refs[2] if is_face else refs[3]

            @pl.when(inside(-dx, -dy))
            def _():
                halo_copy(index, *refs).wait_recv()

            @pl.when(jnp.logical_not(inside(-dx, -dy)))
            def _():
                landed[slot] = jnp.zeros(landed.shape[1:], BF16)

            @pl.when(inside(dx, dy))
            def _():
                halo_copy(index, *refs).wait_send()

    pl.semaphore_wait(barrier, len(greeted))
    u_refs = (send_face, send_diag, halo_face, halo_diag, hu_send, hu_recv)
    halo_start(*u_refs)
    wz_copy = push(w_pair.at[zhi], w_pair.at[zhi], wz_sem.at[0], wz_sem.at[1], partner)
    loads[3].wait()
    take_in(g_ref, field_g, send_gface, send_gdiag)

    wz_copy.wait()
    w_parts[core, pos1, pos2] = w_pair[core]
    w1_copies = []
    for k, device in enumerate(peers1):
        w1_copies.append(
            push(
                w_pair.at[core],
                w_parts.at[core, pos1, pos2],
                w1_send.at[k],
                w1_recv.at[k],
                device,
            )
        )
    halo_wait(*u_refs)
    g_refs = (send_gface, send_gdiag, halo_gface, halo_gdiag, hg_send, hg_recv)
    halo_start(*g_refs)

    def code_of(values, dx, dy):
        values = values.astype(F32)
        code = (values[0:1] + 8.0 * dx) * 1024.0 + (values[1:2] + 8.0 * dy) * 32.0 + values[2:3]
        return jnp.where(values[3:4] > 0.5, code, NOWHERE)

    codes = {(0, 0): code_of(meta, 0, 0)}
    for dx, dy in AROUND:
        is_face, slot = face_slot(-dx, -dy)
        codes[(dx, dy)] = code_of(halo_face[slot, 16] if is_face else halo_diag[slot, 4], dx, dy)
    own_place = (place[0:1] * 1024.0 + place[1:2] * 32.0 + place[2:3])[:, :NB]
    diagonal = iota((NB, NB), 0) == iota((NB, NB), 1)
    own_code = jnp.sum(jnp.where(diagonal, own_place, 0.0), axis=1, keepdims=True)

    picks = {}
    for ax in (-1, 0, 1):
        for ay in (-1, 0, 1):
            tiles = [(dx, dy) for dx in ((0, ax) if ax else (0,)) for dy in ((0, ay) if ay else (0,))]
            depth = NB * len(tiles)
            group = iota((1, depth), 1) // NB
            code_row = codes[tiles[0]][:, :depth]
            for n in range(1, len(tiles)):
                code_row = jnp.where(group == n, codes[tiles[n]][:, :depth], code_row)
            matches = []
            for oz in (-1, 0, 1):
                for ox, oy in tiles:
                    wanted = own_code + float(ox * 1024 + oy * 32 + oz)
                    matches.append(jnp.where(wanted == code_row, 1.0, 0.0))
            picks[(ax, ay)] = (tiles, jnp.concatenate(matches, axis=0).astype(BF16))

    def padded(cell, shift):
        return 0 if shift < 0 else (5 if shift > 0 else cell + 1)

    def assemble(field, faces, diags):
        def source(dx, dy, i, j, k):
            if dx == 0 and dy == 0:
                return field[i + 1, j + 1, k + 1]
            is_face, slot = face_slot(-dx, -dy)
            if not is_face:
                return diags[slot, k]
            return faces[slot, (j if dy == 0 else i) * 4 + k]

        for (ax, ay), (tiles, pick) in picks.items():
            count = len(tiles)
            for i in {-1: (3,), 0: (1, 2), 1: (0,)}[ax]:
                for j in {-1: (3,), 0: (1, 2), 1: (0,)}[ay]:
                    for k in range(4):
                        shifts = {0: (0, 1), 3: (-1, 0)}.get(k, (0,))
                        if count == 1 and k in (1, 2):
                            continue
                        first = (shifts[0] + 1) * count * NB
                        last = (shifts[-1] + 2) * count * NB
                        pool = [source(dx, dy, i, j, k) for dx, dy in tiles]
                        pool = pool[0] if count == 1 else jnp.concatenate(pool, axis=0)
                        got = exact_dot(pick[first:last], pool).astype(BF16)
                        row = 0
                        for oz in shifts:
                            for ox, oy in tiles:
                                if ox or oy or oz:
                                    to = padded(i, ox), padded(j, oy), padded(k, oz)
                                    field[to] = got[row : row + NB]
                                row += NB

    assemble(field_u, halo_face, halo_diag)

    def window(field, tap):
        a, b, e = tap // 9, tap // 3 % 3, tap % 3
        return field[a : a + 4, b : b + 4, e : e + 4].reshape(1024, CH)

    kept = field_g[1:5, 1:5, 1:5].reshape(1024, CH)
    dw_full[TAPS * CH :] = jnp.zeros((dw_full.shape[0] - TAPS * CH, CH), F32)

    def gradient(first, last):
        for tap in range(first, last):
            dw_full[tap * CH : (tap + 1) * CH] = lax.dot_general(
                window(field_u, tap), kept, (((0,), (0,)), ((), ())), preferred_element_type=F32
            )

    def split(which):
        for n in range(plane):
            for part in range(2):
                start = (which * plane + n) * rows + part * half
                nx, ny = n % side, n // side
                to = (nx, ny) if part == 0 else (ny, nx)
                dw_parts[part, which, to[0], to[1]] = dw_full[start : start + half_pad]
        return push(
            dw_parts.at[1 - core, which],
            swap_in.at[which],
            r0_send.at[which],
            r0_recv.at[which],
            sibling,
        )

    def phase_one(which, swap):
        swap.wait()
        chip_sum[which] = dw_parts[core, which] + swap_in[which]
        copies = []
        for k, device in enumerate(peers1):
            index = which * (side - 1) + k
            copies.append(
                push(
                    chip_sum.at[which, ones[k]],
                    one_in.at[which, k],
                    r1_send.at[index],
                    r1_recv.at[index],
                    device,
                )
            )
        return copies

    def phase_two(which, arriving):
        for copy in arriving:
            copy.wait()
        total = chip_sum[which, pos1]
        for k in range(side - 1):
            total = total + one_in[which, k]
        one_sum[which] = total
        copies = []
        for k, device in enumerate(peers2):
            index = which * (side - 1) + k
            copies.append(
                push(
                    one_sum.at[which, twos[k]],
                    two_in.at[which, k],
                    r2_send.at[index],
                    r2_recv.at[index],
                    device,
                )
            )
        return copies

    def phase_done(which, arriving):
        for copy in arriving:
            copy.wait()
        total = one_sum[which, pos2]
        for k in range(side - 1):
            total = total + two_in[which, k]
        plane_sum[which] = total

    gradient(0, 14)
    swap_low = split(0)
    for copy in w1_copies:
        copy.wait()
    w2_copies = []
    for k, device in enumerate(peers2):
        w2_copies.append(
            push(
                w_parts.at[core, :, pos2],
                w_parts.at[core, :, pos2],
                w2_send.at[k],
                w2_recv.at[k],
                device,
            )
        )
    gradient(14, TAPS)
    swap_high = split(1)
    one_low = phase_one(0, swap_low)
    one_high = phase_one(1, swap_high)
    for copy in w2_copies:
        copy.wait()
    ws_copy = push(w_parts.at[core], w_parts.at[core], ws_sem.at[0], ws_sem.at[1], sibling)
    halo_wait(*g_refs)
    assemble(field_g, halo_gface, halo_gdiag)
    ws_copy.wait()
    for which in range(2):
        for n in range(plane):
            nx, ny = n % side, n // side
            to = (nx, ny) if which == 0 else (ny, nx)
            start = (which * plane + n) * rows
            w_full[start : start + rows] = w_parts[which, to[0], to[1], 0:rows]
    for tap in range(TAPS):
        w_turned[(26 - tap) * CH : (27 - tap) * CH] = w_full[tap * CH : (tap + 1) * CH].T

    def convolve(field, weights, result_ref, i):
        total = None
        for tap in range(0, TAPS, 2):
            last = min(tap + 2, TAPS)
            left = []
            for n in range(tap, last):
                a, b, e = n // 9, n // 3 % 3, n % 3
                left.append(field[i + a, b : b + 4, e : e + 4].reshape(256, CH))
            left = left[0] if len(left) == 1 else jnp.concatenate(left, axis=1)
            term = exact_dot(left, weights[tap * CH : last * CH])
            total = term if total is None else total + term
        slab = exact_dot(turn_out, total.astype(BF16)).astype(BF16)
        result_ref[0, :, 16 * i : 16 * i + 16, :] = slab.reshape(NB, 16, CH)

    for i in range(4):
        convolve(field_u, w_full, out_ref, i)
    two_low = phase_two(0, one_low)
    two_high = phase_two(1, one_high)
    for i in range(2):
        convolve(field_g, w_turned, gf_ref, i)
    phase_done(0, two_low)
    phase_done(1, two_high)

    def piece_start(low):
        start = low * piece
        return pl.multiple_of(jnp.minimum(start, half_pad - piece), 8)

    z_copies = []
    for k, device in enumerate(z_peers):
        low = lax.rem(zeds[k], z_low)
        z_copies.append(
            push(
                plane_sum.at[zeds[k] // z_low, pl.ds(piece_start(low), piece)],
                z_in.at[k],
                r3_send.at[k],
                r3_recv.at[k],
                device,
            )
        )
    for i in range(2, 4):
        convolve(field_g, w_turned, gf_ref, i)
    for copy in z_copies:
        copy.wait()
    total = plane_sum[zhi, pl.ds(piece_start(zlo), piece)]
    for k in range(z_all - 1):
        total = total + z_in[k]
    pieces[p] = total * (1.0 / math.sqrt(gx_size * gy_size * NB * 64))
    last_copies = []
    for k, device in enumerate(gx_peers):
        last_copies.append(push(pieces.at[p], pieces.at[p], r4_send.at[k], r4_recv.at[k], device))
    for copy in last_copies:
        copy.wait()
    for n in range(gx_size):
        part, low = n % 2, n // 2
        start = min(low * piece, half_pad - piece)
        count = min(piece, half - start)
        gw_ref[part * half + start : part * half + start + count] = pieces[n, 0:count]


def local(gx_size, gy_size, features, block_at, block_coords, weight, cotangent):
    plane = gy_size // 2
    side = math.isqrt(plane)
    z_low = gx_size // 2
    z_all = 2 * z_low
    rows = TAPS * CH // gy_size
    rows_pad = -(-rows // 16) * 16
    half_pad = -(-(rows // 2) // 8) * 8
    piece = -(-half_pad // (8 * z_low)) * 8
    blocks = pl.BlockSpec(memory_space=pltpu.VMEM)
    vmem = pltpu.VMEM
    dma = pltpu.SemaphoreType.DMA
    positions = block_at.reshape(-1, block_at.shape[2])
    return pl.pallas_call(
        functools.partial(kernel, gx_size, gy_size, side),
        out_shape=(
            jax.ShapeDtypeStruct(features.shape, BF16),
            jax.ShapeDtypeStruct(features.shape, BF16),
            jax.ShapeDtypeStruct((rows, CH), F32),
        ),
        in_specs=[pl.BlockSpec(memory_space=pl.ANY)] * 5,
        out_specs=[blocks] * 3,
        scratch_shapes=[
            vmem(features.shape, BF16),
            vmem(positions.shape, jnp.int32),
            vmem(block_coords.shape, jnp.int32),
            vmem(weight.shape, BF16),
            vmem(features.shape, BF16),
            vmem((6, 6, 6, NB, CH), BF16),
            vmem((6, 6, 6, NB, CH), BF16),
            vmem((4, 17, NB, CH), BF16),
            vmem((4, 5, NB, CH), BF16),
            vmem((4, 17, NB, CH), BF16),
            vmem((4, 5, NB, CH), BF16),
            vmem((4, 16, NB, CH), BF16),
            vmem((4, 4, NB, CH), BF16),
            vmem((4, 16, NB, CH), BF16),
            vmem((4, 4, NB, CH), BF16),
            vmem((2, rows_pad, CH), BF16),
            vmem((2, side, side, rows_pad, CH), BF16),
            vmem((TAPS * CH, CH), BF16),
            vmem((TAPS * CH, CH), BF16),
            vmem((TAPS * CH + 16, CH), F32),
            vmem((2, 2, side, side, half_pad, CH), F32),
            vmem((2, side, side, half_pad, CH), F32),
            vmem((2, side, side, half_pad, CH), F32),
            vmem((2, side - 1, side, half_pad, CH), F32),
            vmem((2, side, half_pad, CH), F32),
            vmem((2, side - 1, half_pad, CH), F32),
            vmem((2, half_pad, CH), F32),
            vmem((z_all - 1, piece, CH), F32),
            vmem((gx_size, piece, CH), F32),
            dma((5,)),
            dma((8,)),
            dma((8,)),
            dma((8,)),
            dma((8,)),
            dma((2,)),
            dma((side - 1,)),
            dma((side - 1,)),
            dma((side - 1,)),
            dma((side - 1,)),
            dma((2,)),
            dma((2,)),
            dma((2,)),
            dma((2 * side - 2,)),
            dma((2 * side - 2,)),
            dma((2 * side - 2,)),
            dma((2 * side - 2,)),
            dma((z_all - 1,)),
            dma((z_all - 1,)),
            dma((gx_size - 1,)),
            dma((gx_size - 1,)),
        ],
        compiler_params=pltpu.CompilerParams(
            collective_id=0, has_side_effects=True, vmem_limit_bytes=48 * 1024 * 1024
        ),
    )(features, positions, block_coords, weight, cotangent)


def solution(mesh):
    placed = (
        P("gx", "gy", None, None),
        P("gx", "gy", None),
        P("gx", None, "gy"),
        P("gy", None),
        P("gx", "gy", None, None),
    )
    return jax.shard_map(
        functools.partial(local, mesh.shape["gx"], mesh.shape["gy"]),
        mesh=mesh,
        in_specs=placed,
        out_specs=(P("gx", "gy", None, None), P("gx", "gy", None, None), P("gy", None)),
        check_vma=False,
    )
```

```python
import functools
import math

import jax
import jax.numpy as jnp
from jax import lax
from jax.experimental import pallas as pl
from jax.experimental.pallas import tpu as pltpu
from jax.sharding import PartitionSpec as P

MESH = pl.DeviceIdType.MESH
F32 = jnp.float32
BF16 = jnp.bfloat16
CH = 128
NB = 16
TAPS = 27
NOWHERE = -1.0e6
AROUND = [(dx, dy) for dx in (-1, 0, 1) for dy in (-1, 0, 1) if dx or dy]


def iota(shape, dim):
    return lax.broadcasted_iota(jnp.int32, shape, dim)


def zero_one(mask):
    return jnp.where(mask, 1.0, 0.0).astype(BF16)


def exact_dot(left, right):
    return jnp.dot(left, right, preferred_element_type=F32)


def face_slot(dx, dy):
    if dy == 0:
        return True, 0 if dx > 0 else 1
    if dx == 0:
        return True, 2 if dy > 0 else 3
    return False, (0 if dx > 0 else 2) + (0 if dy > 0 else 1)


def kernel(
    gx_size,
    gy_size,
    side,
    f_hbm,
    at_hbm,
    coords_hbm,
    w_hbm,
    g_hbm,
    out_ref,
    gf_ref,
    gw_ref,
    f_ref,
    at_ref,
    coords_ref,
    w_ref,
    g_ref,
    field_u,
    field_g,
    send_face,
    send_diag,
    halo_face,
    halo_diag,
    send_gface,
    send_gdiag,
    halo_gface,
    halo_gdiag,
    w_pair,
    w_parts,
    w_full,
    w_turned,
    dw_full,
    dw_parts,
    swap_in,
    chip_sum,
    one_in,
    one_sum,
    two_in,
    plane_sum,
    z_in,
    pieces,
    in_sem,
    hu_send,
    hu_recv,
    hg_send,
    hg_recv,
    wz_sem,
    wp_send,
    wp_recv,
    ws_sem,
    r0_send,
    r0_recv,
    r1_send,
    r1_recv,
    r2_send,
    r2_recv,
    r3_send,
    r3_recv,
    r4_send,
    r4_recv,
):
    plane = side * side
    z_low = gx_size // 2
    z_all = 2 * z_low
    rows = TAPS * CH // gy_size
    half = rows // 2
    half_pad = plane_sum.shape[1]
    piece = pieces.shape[1]
    p = lax.axis_index("gx")
    q = lax.axis_index("gy")
    core = lax.rem(p, 2)
    zlo = p // 2
    zhi = q // plane
    spot = lax.rem(q, plane)
    zed = zhi * z_low + zlo
    x = lax.rem(spot, side)
    y = spot // side
    pos1 = x + core * (y - x)
    pos2 = y + core * (x - y)
    step1 = 1 + core * (side - 1)
    step2 = side - core * (side - 1)

    sibling = (p + 1 - 2 * core, q)
    partner = (p, spot + (1 - zhi) * plane)
    ones = [lax.rem(pos1 + k, side) for k in range(1, side)]
    twos = [lax.rem(pos2 + k, side) for k in range(1, side)]
    peers1 = [(p, zhi * plane + n * step1 + pos2 * step2) for n in ones]
    peers2 = [(p, zhi * plane + pos1 * step1 + n * step2) for n in twos]
    plane_peers = []
    for k in range(1, plane):
        n1, n2 = lax.rem(pos1 + k % side, side), lax.rem(pos2 + k // side, side)
        plane_peers.append((p, zhi * plane + n1 * step1 + n2 * step2))
    zeds = [lax.rem(zed + k, z_all) for k in range(1, z_all)]
    z_peers = [(lax.rem(z, z_low) * 2 + core, (z // z_low) * plane + spot) for z in zeds]
    gx_peers = [(lax.rem(p + k, gx_size), q) for k in range(1, gx_size)]

    def at(dx, dy):
        return (lax.rem(p + dx + gx_size, gx_size), lax.rem(q + dy + gy_size, gy_size))

    def inside(dx, dy):
        return (p + dx >= 0) & (p + dx < gx_size) & (q + dy >= 0) & (q + dy < gy_size)

    barrier = pltpu.get_barrier_semaphore()
    greeted = [sibling, partner] + plane_peers + z_peers + gx_peers
    greeted = greeted + [at(dx, dy) for dx, dy in AROUND]
    for device in greeted:
        pl.semaphore_signal(barrier, inc=1, device_id=device, device_id_type=MESH)
    loads = []
    pairs = ((at_hbm, at_ref), (coords_hbm, coords_ref), (f_hbm, f_ref), (g_hbm, g_ref), (w_hbm, w_ref))
    for index, (src, dst) in enumerate(pairs):
        copy = pltpu.make_async_copy(src, dst, in_sem.at[index])
        copy.start()
        loads.append(copy)

    loads[0].wait()
    loads[1].wait()
    lane_slot = lax.rem(iota((1, CH), 1), NB).astype(F32)
    found = jnp.zeros((at_ref.shape[0], CH), F32)
    placed = at_ref[...].astype(F32)
    for z in range(placed.shape[1]):
        found = jnp.maximum(found, jnp.where(placed[:, z : z + 1] == lane_slot, 1.0, 0.0))
    live = jnp.max(found, axis=0, keepdims=True)
    spread = zero_one(lax.rem(iota((NB, CH), 1), NB) == iota((NB, CH), 0))
    coords = coords_ref[:, 0, :].astype(F32).astype(BF16)
    place = exact_dot(coords, spread)
    meta = jnp.concatenate([place, live, jnp.zeros((NB - 4, CH), F32)], axis=0).astype(BF16)

    live_rows = jnp.broadcast_to(live[:, :NB], (8, NB)).astype(BF16)
    by_high = zero_one(iota((NB, NB * NB), 1) // NB == iota((NB, NB * NB), 0))
    by_low = zero_one(lax.rem(iota((NB, NB * NB), 1), NB) == iota((NB, NB * NB), 0))
    live_high = exact_dot(live_rows, by_high)[0:1]
    live_low = exact_dot(live_rows, by_low)[0:1]
    row_id = iota((NB * NB, NB * NB), 0)
    col_id = iota((NB * NB, NB * NB), 1)
    turned = (lax.rem(row_id, NB) == col_id // NB) & (row_id // NB == lax.rem(col_id, NB))
    turn = jnp.where(turned, 1.0, 0.0)
    turn_in = (turn * live_high).astype(BF16)
    turn_out = (turn * live_low).astype(BF16)

    def take_in(ref, field, faces, diags):
        for i in range(4):
            block = ref[0, :, 16 * i : 16 * i + 16, :].reshape(NB * NB, CH)
            slab = exact_dot(turn_in, block).astype(BF16).reshape(4, 4, NB, CH)
            field[i + 1, 1:5, 1:5] = slab
            for which, along in ((0, 3), (1, 0)):
                if i == along:
                    faces[which, 0:16] = slab.reshape(16, NB, CH)
                    diags[2 * which, 0:4] = slab[3]
                    diags[2 * which + 1, 0:4] = slab[0]
            faces[2, 4 * i : 4 * i + 4] = slab[3]
            faces[3, 4 * i : 4 * i + 4] = slab[0]

    loads[2].wait()
    take_in(f_ref, field_u, send_face, send_diag)
    for n in range(4):
        send_face[n, 16] = meta
        send_diag[n, 4] = meta
    loads[4].wait()
    w_pair[zhi] = jnp.zeros((w_pair.shape[1], CH), BF16)
    w_pair[zhi, 0:rows] = w_ref[...]

    def remote(src, dst, send_sem, recv_sem, device):
        return pltpu.make_async_remote_copy(
            src_ref=src,
            dst_ref=dst,
            send_sem=send_sem,
            recv_sem=recv_sem,
            device_id=device,
            device_id_type=MESH,
        )

    def push(src, dst, send_sem, recv_sem, device):
        copy = remote(src, dst, send_sem, recv_sem, device)
        copy.start()
        return copy

    def halo_copy(index, faces, diags, faces_in, diags_in, send_sem, recv_sem):
        dx, dy = AROUND[index]
        is_face, slot = face_slot(dx, dy)
        src = faces.at[slot] if is_face else diags.at[slot]
        dst = faces_in.at[slot] if is_face else diags_in.at[slot]
        return remote(src, dst, send_sem.at[index], recv_sem.at[index], at(dx, dy))

    def halo_start(*refs):
        for index, (dx, dy) in enumerate(AROUND):

            @pl.when(inside(dx, dy))
            def _():
                halo_copy(index, *refs).start()

    def halo_wait(*refs):
        for index, (dx, dy) in enumerate(AROUND):
            is_face, slot = face_slot(dx, dy)
            landed = refs[2] if is_face else refs[3]

            @pl.when(inside(-dx, -dy))
            def _():
                halo_copy(index, *refs).wait_recv()

            @pl.when(jnp.logical_not(inside(-dx, -dy)))
            def _():
                landed[slot] = jnp.zeros(landed.shape[1:], BF16)

            @pl.when(inside(dx, dy))
            def _():
                halo_copy(index, *refs).wait_send()

    pl.semaphore_wait(barrier, len(greeted))
    u_refs = (send_face, send_diag, halo_face, halo_diag, hu_send, hu_recv)
    wz_copy = push(w_pair.at[zhi], w_pair.at[zhi], wz_sem.at[0], wz_sem.at[1], partner)
    halo_start(*u_refs)
    loads[3].wait()
    take_in(g_ref, field_g, send_gface, send_gdiag)

    wz_copy.wait()
    w_parts[core, pos1, pos2] = w_pair[core]
    w_copies = []
    for k, device in enumerate(plane_peers):
        w_copies.append(
            push(
                w_pair.at[core], w_parts.at[core, pos1, pos2], wp_send.at[k], wp_recv.at[k], device
            )
        )

    halo_wait(*u_refs)
    g_refs = (send_gface, send_gdiag, halo_gface, halo_gdiag, hg_send, hg_recv)

    def code_of(values, dx, dy):
        values = values.astype(F32)
        code = (values[0:1] + 8.0 * dx) * 1024.0 + (values[1:2] + 8.0 * dy) * 32.0 + values[2:3]
        return jnp.where(values[3:4] > 0.5, code, NOWHERE)

    codes = {(0, 0): code_of(meta, 0, 0)}
    for dx, dy in AROUND:
        is_face, slot = face_slot(-dx, -dy)
        codes[(dx, dy)] = code_of(halo_face[slot, 16] if is_face else halo_diag[slot, 4], dx, dy)
    own_place = (place[0:1] * 1024.0 + place[1:2] * 32.0 + place[2:3])[:, :NB]
    diagonal = iota((NB, NB), 0) == iota((NB, NB), 1)
    own_code = jnp.sum(jnp.where(diagonal, own_place, 0.0), axis=1, keepdims=True)

    picks = {}
    for ax in (-1, 0, 1):
        for ay in (-1, 0, 1):
            tiles = [(dx, dy) for dx in ((0, ax) if ax else (0,)) for dy in ((0, ay) if ay else (0,))]
            depth = NB * len(tiles)
            group = iota((1, depth), 1) // NB
            code_row = codes[tiles[0]][:, :depth]
            for n in range(1, len(tiles)):
                code_row = jnp.where(group == n, codes[tiles[n]][:, :depth], code_row)
            matches = []
            for oz in (-1, 0, 1):
                for ox, oy in tiles:
                    wanted = own_code + float(ox * 1024 + oy * 32 + oz)
                    matches.append(jnp.where(wanted == code_row, 1.0, 0.0))
            picks[(ax, ay)] = (tiles, jnp.concatenate(matches, axis=0).astype(BF16))

    def padded(cell, shift):
        return 0 if shift < 0 else (5 if shift > 0 else cell + 1)

    def assemble(field, faces, diags):
        def source(dx, dy, i, j, k):
            if dx == 0 and dy == 0:
                return field[i + 1, j + 1, k + 1]
            is_face, slot = face_slot(-dx, -dy)
            if not is_face:
                return diags[slot, k]
            return faces[slot, (j if dy == 0 else i) * 4 + k]

        for (ax, ay), (tiles, pick) in picks.items():
            count = len(tiles)
            for i in {-1: (3,), 0: (1, 2), 1: (0,)}[ax]:
                for j in {-1: (3,), 0: (1, 2), 1: (0,)}[ay]:
                    for k in range(4):
                        shifts = {0: (0, 1), 3: (-1, 0)}.get(k, (0,))
                        if count == 1 and k in (1, 2):
                            continue
                        first = (shifts[0] + 1) * count * NB
                        last = (shifts[-1] + 2) * count * NB
                        pool = [source(dx, dy, i, j, k) for dx, dy in tiles]
                        pool = pool[0] if count == 1 else jnp.concatenate(pool, axis=0)
                        got = exact_dot(pick[first:last], pool).astype(BF16)
                        row = 0
                        for oz in shifts:
                            for ox, oy in tiles:
                                if ox or oy or oz:
                                    to = padded(i, ox), padded(j, oy), padded(k, oz)
                                    field[to] = got[row : row + NB]
                                row += NB

    assemble(field_u, halo_face, halo_diag)

    def window(field, tap):
        a, b, e = tap // 9, tap // 3 % 3, tap % 3
        return field[a : a + 4, b : b + 4, e : e + 4].reshape(1024, CH)

    kept = field_g[1:5, 1:5, 1:5].reshape(1024, CH)
    dw_full[TAPS * CH :] = jnp.zeros((dw_full.shape[0] - TAPS * CH, CH), F32)

    def gradient(first, last):
        for tap in range(first, last):
            dw_full[tap * CH : (tap + 1) * CH] = lax.dot_general(
                window(field_u, tap), kept, (((0,), (0,)), ((), ())), preferred_element_type=F32
            )

    def split(which):
        for n in range(plane):
            for part in range(2):
                start = (which * plane + n) * rows + part * half
                nx, ny = n % side, n // side
                to = (nx, ny) if part == 0 else (ny, nx)
                dw_parts[part, which, to[0], to[1]] = dw_full[start : start + half_pad]
        return push(
            dw_parts.at[1 - core, which],
            swap_in.at[which],
            r0_send.at[which],
            r0_recv.at[which],
            sibling,
        )

    def phase_one(which, swap):
        swap.wait()
        chip_sum[which] = dw_parts[core, which] + swap_in[which]
        copies = []
        for k, device in enumerate(peers1):
            index = which * (side - 1) + k
            copies.append(
                push(
                    chip_sum.at[which, ones[k]],
                    one_in.at[which, k],
                    r1_send.at[index],
                    r1_recv.at[index],
                    device,
                )
            )
        return copies

    def phase_two(which, arriving):
        for copy in arriving:
            copy.wait()
        total = chip_sum[which, pos1]
        for k in range(side - 1):
            total = total + one_in[which, k]
        one_sum[which] = total
        copies = []
        for k, device in enumerate(peers2):
            index = which * (side - 1) + k
            copies.append(
                push(
                    one_sum.at[which, twos[k]],
                    two_in.at[which, k],
                    r2_send.at[index],
                    r2_recv.at[index],
                    device,
                )
            )
        return copies

    def phase_done(which, arriving):
        for copy in arriving:
            copy.wait()
        total = one_sum[which, pos2]
        for k in range(side - 1):
            total = total + two_in[which, k]
        plane_sum[which] = total

    gradient(0, 14)
    swap_low = split(0)
    gradient(14, TAPS)
    swap_high = split(1)
    one_low = phase_one(0, swap_low)
    one_high = phase_one(1, swap_high)
    halo_start(*g_refs)
    for copy in w_copies:
        copy.wait()
    ws_copy = push(w_parts.at[core], w_parts.at[core], ws_sem.at[0], ws_sem.at[1], sibling)
    ws_copy.wait()
    for which in range(2):
        for n in range(plane):
            nx, ny = n % side, n // side
            to = (nx, ny) if which == 0 else (ny, nx)
            start = (which * plane + n) * rows
            w_full[start : start + rows] = w_parts[which, to[0], to[1], 0:rows]
    for tap in range(TAPS):
        w_turned[(26 - tap) * CH : (27 - tap) * CH] = w_full[tap * CH : (tap + 1) * CH].T

    def convolve(field, weights, result_ref, i):
        total = None
        for tap in range(0, TAPS, 2):
            last = min(tap + 2, TAPS)
            left = []
            for n in range(tap, last):
                a, b, e = n // 9, n // 3 % 3, n % 3
                left.append(field[i + a, b : b + 4, e : e + 4].reshape(256, CH))
            left = left[0] if len(left) == 1 else jnp.concatenate(left, axis=1)
            term = exact_dot(left, weights[tap * CH : last * CH])
            total = term if total is None else total + term
        slab = exact_dot(turn_out, total.astype(BF16)).astype(BF16)
        result_ref[0, :, 16 * i : 16 * i + 16, :] = slab.reshape(NB, 16, CH)

    for i in range(2):
        convolve(field_u, w_full, out_ref, i)
    two_low = phase_two(0, one_low)
    two_high = phase_two(1, one_high)
    for i in range(2, 4):
        convolve(field_u, w_full, out_ref, i)
    halo_wait(*g_refs)
    assemble(field_g, halo_gface, halo_gdiag)
    phase_done(0, two_low)
    phase_done(1, two_high)

    def piece_start(low):
        start = low * piece
        return pl.multiple_of(jnp.minimum(start, half_pad - piece), 8)

    z_copies = []
    for k, device in enumerate(z_peers):
        low = lax.rem(zeds[k], z_low)
        z_copies.append(
            push(
                plane_sum.at[zeds[k] // z_low, pl.ds(piece_start(low), piece)],
                z_in.at[k],
                r3_send.at[k],
                r3_recv.at[k],
                device,
            )
        )
    for i in range(0, 2):
        convolve(field_g, w_turned, gf_ref, i)
    for copy in z_copies:
        copy.wait()
    total = plane_sum[zhi, pl.ds(piece_start(zlo), piece)]
    for k in range(z_all - 1):
        total = total + z_in[k]
    pieces[p] = total * (1.0 / math.sqrt(gx_size * gy_size * NB * 64))
    last_copies = []
    for k, device in enumerate(gx_peers):
        last_copies.append(push(pieces.at[p], pieces.at[p], r4_send.at[k], r4_recv.at[k], device))
    for i in range(2, 4):
        convolve(field_g, w_turned, gf_ref, i)
    for copy in last_copies:
        copy.wait()
    for n in range(gx_size):
        part, low = n % 2, n // 2
        start = min(low * piece, half_pad - piece)
        count = min(piece, half - start)
        gw_ref[part * half + start : part * half + start + count] = pieces[n, 0:count]


def deliver(a_ref, b_ref, c_ref, a_out, b_out, c_out):
    a_out[...] = a_ref[...]
    b_out[...] = b_ref[...]
    c_out[...] = c_ref[...]


def hand_over(*arrays):
    return pl.pallas_call(
        deliver,
        out_shape=tuple(jax.ShapeDtypeStruct(a.shape, a.dtype) for a in arrays),
        in_specs=[pl.BlockSpec(memory_space=pltpu.VMEM)] * 3,
        out_specs=[pl.BlockSpec(memory_space=pltpu.VMEM)] * 3,
    )(*arrays)


def local(gx_size, gy_size, features, block_at, block_coords, weight, cotangent):
    plane = gy_size // 2
    side = math.isqrt(plane)
    z_low = gx_size // 2
    z_all = 2 * z_low
    rows = TAPS * CH // gy_size
    rows_pad = -(-rows // 16) * 16
    half_pad = -(-(rows // 2) // 8) * 8
    piece = -(-half_pad // (8 * z_low)) * 8
    blocks = pl.BlockSpec(memory_space=pltpu.VMEM)
    vmem = pltpu.VMEM
    dma = pltpu.SemaphoreType.DMA
    corners = block_coords.transpose(1, 0, 2)
    positions = block_at.reshape(-1, block_at.shape[2])
    results = pl.pallas_call(
        functools.partial(kernel, gx_size, gy_size, side),
        out_shape=(
            jax.ShapeDtypeStruct(features.shape, BF16),
            jax.ShapeDtypeStruct(features.shape, BF16),
            jax.ShapeDtypeStruct((rows, CH), F32),
        ),
        in_specs=[pl.BlockSpec(memory_space=pl.ANY)] * 5,
        out_specs=[blocks] * 3,
        scratch_shapes=[
            vmem(features.shape, BF16),
            vmem(positions.shape, jnp.int32),
            vmem(corners.shape, jnp.int32),
            vmem(weight.shape, BF16),
            vmem(features.shape, BF16),
            vmem((6, 6, 6, NB, CH), BF16),
            vmem((6, 6, 6, NB, CH), BF16),
            vmem((4, 17, NB, CH), BF16),
            vmem((4, 5, NB, CH), BF16),
            vmem((4, 17, NB, CH), BF16),
            vmem((4, 5, NB, CH), BF16),
            vmem((4, 16, NB, CH), BF16),
            vmem((4, 4, NB, CH), BF16),
            vmem((4, 16, NB, CH), BF16),
            vmem((4, 4, NB, CH), BF16),
            vmem((2, rows_pad, CH), BF16),
            vmem((2, side, side, rows_pad, CH), BF16),
            vmem((TAPS * CH, CH), BF16),
            vmem((TAPS * CH, CH), BF16),
            vmem((TAPS * CH + 16, CH), F32),
            vmem((2, 2, side, side, half_pad, CH), F32),
            vmem((2, side, side, half_pad, CH), F32),
            vmem((2, side, side, half_pad, CH), F32),
            vmem((2, side - 1, side, half_pad, CH), F32),
            vmem((2, side, half_pad, CH), F32),
            vmem((2, side - 1, half_pad, CH), F32),
            vmem((2, half_pad, CH), F32),
            vmem((z_all - 1, piece, CH), F32),
            vmem((gx_size, piece, CH), F32),
            dma((5,)),
            dma((8,)),
            dma((8,)),
            dma((8,)),
            dma((8,)),
            dma((2,)),
            dma((plane - 1,)),
            dma((plane - 1,)),
            dma((2,)),
            dma((2,)),
            dma((2,)),
            dma((2 * side - 2,)),
            dma((2 * side - 2,)),
            dma((2 * side - 2,)),
            dma((2 * side - 2,)),
            dma((z_all - 1,)),
            dma((z_all - 1,)),
            dma((gx_size - 1,)),
            dma((gx_size - 1,)),
        ],
        compiler_params=pltpu.CompilerParams(
            collective_id=0, has_side_effects=True, vmem_limit_bytes=63 * 1024 * 1024
        ),
    )(features, positions, corners, weight, cotangent)
    return hand_over(*results)


def solution(mesh):
    placed = (
        P("gx", "gy", None, None),
        P("gx", "gy", None),
        P("gx", None, "gy"),
        P("gy", None),
        P("gx", "gy", None, None),
    )
    return jax.shard_map(
        functools.partial(local, mesh.shape["gx"], mesh.shape["gy"]),
        mesh=mesh,
        in_specs=placed,
        out_specs=(P("gx", "gy", None, None), P("gx", "gy", None, None), P("gy", None)),
        check_vma=False,
    )
```

```python
import functools
import math

import jax
import jax.numpy as jnp
from jax import lax
from jax.experimental import pallas as pl
from jax.experimental.pallas import tpu as pltpu
from jax.sharding import PartitionSpec as P

MESH = pl.DeviceIdType.MESH
F32 = jnp.float32
BF16 = jnp.bfloat16
CH = 128
NB = 16
TAPS = 27
NOWHERE = -1.0e6
AROUND = [(dx, dy) for dx in (-1, 0, 1) for dy in (-1, 0, 1) if dx or dy]


def iota(shape, dim):
    return lax.broadcasted_iota(jnp.int32, shape, dim)


def zero_one(mask):
    return jnp.where(mask, 1.0, 0.0).astype(BF16)


def exact_dot(left, right):
    return jnp.dot(left, right, preferred_element_type=F32)


def face_slot(dx, dy):
    if dy == 0:
        return True, 0 if dx > 0 else 1
    if dx == 0:
        return True, 2 if dy > 0 else 3
    return False, (0 if dx > 0 else 2) + (0 if dy > 0 else 1)


def kernel(
    gx_size,
    gy_size,
    side,
    f_hbm,
    at_hbm,
    coords_hbm,
    w_hbm,
    g_hbm,
    out_ref,
    gf_ref,
    gw_ref,
    f_ref,
    at_ref,
    coords_ref,
    w_ref,
    g_ref,
    field_u,
    field_g,
    send_face,
    send_diag,
    halo_face,
    halo_diag,
    send_gface,
    send_gdiag,
    halo_gface,
    halo_gdiag,
    w_pair,
    w_parts,
    w_full,
    w_turned,
    dw_full,
    dw_parts,
    swap_in,
    chip_sum,
    one_in,
    one_sum,
    two_in,
    plane_sum,
    z_in,
    pieces,
    in_sem,
    hu_send,
    hu_recv,
    hg_send,
    hg_recv,
    wz_sem,
    wp_send,
    wp_recv,
    ws_sem,
    r0_send,
    r0_recv,
    r1_send,
    r1_recv,
    r2_send,
    r2_recv,
    r3_send,
    r3_recv,
    r4_send,
    r4_recv,
):
    plane = side * side
    z_low = gx_size // 2
    z_all = 2 * z_low
    rows = TAPS * CH // gy_size
    half = rows // 2
    half_pad = plane_sum.shape[1]
    piece = pieces.shape[1]
    p = lax.axis_index("gx")
    q = lax.axis_index("gy")
    core = lax.rem(p, 2)
    zlo = p // 2
    zhi = q // plane
    spot = lax.rem(q, plane)
    zed = zhi * z_low + zlo
    x = lax.rem(spot, side)
    y = spot // side
    pos1 = x + core * (y - x)
    pos2 = y + core * (x - y)
    step1 = 1 + core * (side - 1)
    step2 = side - core * (side - 1)

    sibling = (p + 1 - 2 * core, q)
    partner = (p, spot + (1 - zhi) * plane)
    ones = [lax.rem(pos1 + k, side) for k in range(1, side)]
    twos = [lax.rem(pos2 + k, side) for k in range(1, side)]
    peers1 = [(p, zhi * plane + n * step1 + pos2 * step2) for n in ones]
    peers2 = [(p, zhi * plane + pos1 * step1 + n * step2) for n in twos]
    plane_peers = []
    for k in range(1, plane):
        n1, n2 = lax.rem(pos1 + k % side, side), lax.rem(pos2 + k // side, side)
        plane_peers.append((p, zhi * plane + n1 * step1 + n2 * step2))
    zeds = [lax.rem(zed + k, z_all) for k in range(1, z_all)]
    z_peers = [(lax.rem(z, z_low) * 2 + core, (z // z_low) * plane + spot) for z in zeds]
    gx_peers = [(lax.rem(p + k, gx_size), q) for k in range(1, gx_size)]

    def at(dx, dy):
        return (lax.rem(p + dx + gx_size, gx_size), lax.rem(q + dy + gy_size, gy_size))

    def inside(dx, dy):
        return (p + dx >= 0) & (p + dx < gx_size) & (q + dy >= 0) & (q + dy < gy_size)

    barrier = pltpu.get_barrier_semaphore()
    greeted = [sibling, partner] + plane_peers + z_peers + gx_peers
    greeted = greeted + [at(dx, dy) for dx, dy in AROUND]
    for device in greeted:
        pl.semaphore_signal(barrier, inc=1, device_id=device, device_id_type=MESH)
    loads = []
    pairs = ((at_hbm, at_ref), (coords_hbm, coords_ref), (f_hbm, f_ref), (g_hbm, g_ref), (w_hbm, w_ref))
    for index, (src, dst) in enumerate(pairs):
        copy = pltpu.make_async_copy(src, dst, in_sem.at[index])
        copy.start()
        loads.append(copy)

    loads[0].wait()
    loads[1].wait()
    lane_slot = lax.rem(iota((1, CH), 1), NB).astype(F32)
    found = jnp.zeros((at_ref.shape[0], CH), F32)
    placed = at_ref[...].astype(F32)
    for z in range(placed.shape[1]):
        found = jnp.maximum(found, jnp.where(placed[:, z : z + 1] == lane_slot, 1.0, 0.0))
    live = jnp.max(found, axis=0, keepdims=True)
    spread = zero_one(lax.rem(iota((NB, CH), 1), NB) == iota((NB, CH), 0))
    coords = coords_ref[:, 0, :].astype(F32).astype(BF16)
    place = exact_dot(coords, spread)
    meta = jnp.concatenate([place, live, jnp.zeros((NB - 4, CH), F32)], axis=0).astype(BF16)

    live_rows = jnp.broadcast_to(live[:, :NB], (8, NB)).astype(BF16)
    by_high = zero_one(iota((NB, NB * NB), 1) // NB == iota((NB, NB * NB), 0))
    by_low = zero_one(lax.rem(iota((NB, NB * NB), 1), NB) == iota((NB, NB * NB), 0))
    live_high = exact_dot(live_rows, by_high)[0:1]
    live_low = exact_dot(live_rows, by_low)[0:1]
    row_id = iota((NB * NB, NB * NB), 0)
    col_id = iota((NB * NB, NB * NB), 1)
    turned = (lax.rem(row_id, NB) == col_id // NB) & (row_id // NB == lax.rem(col_id, NB))
    turn = jnp.where(turned, 1.0, 0.0)
    turn_in = (turn * live_high).astype(BF16)
    turn_out = (turn * live_low).astype(BF16)

    def take_in(ref, field, faces, diags):
        for i in range(4):
            block = ref[0, :, 16 * i : 16 * i + 16, :].reshape(NB * NB, CH)
            slab = exact_dot(turn_in, block).astype(BF16).reshape(4, 4, NB, CH)
            field[i + 1, 1:5, 1:5] = slab
            for which, along in ((0, 3), (1, 0)):
                if i == along:
                    faces[which, 0:16] = slab.reshape(16, NB, CH)
                    diags[2 * which, 0:4] = slab[3]
                    diags[2 * which + 1, 0:4] = slab[0]
            faces[2, 4 * i : 4 * i + 4] = slab[3]
            faces[3, 4 * i : 4 * i + 4] = slab[0]

    loads[2].wait()
    take_in(f_ref, field_u, send_face, send_diag)
    for n in range(4):
        send_face[n, 16] = meta
        send_diag[n, 4] = meta
    loads[4].wait()
    w_pair[zhi] = jnp.zeros((w_pair.shape[1], CH), BF16)
    w_pair[zhi, 0:rows] = w_ref[...]

    def remote(src, dst, send_sem, recv_sem, device):
        return pltpu.make_async_remote_copy(
            src_ref=src,
            dst_ref=dst,
            send_sem=send_sem,
            recv_sem=recv_sem,
            device_id=device,
            device_id_type=MESH,
        )

    def push(src, dst, send_sem, recv_sem, device):
        copy = remote(src, dst, send_sem, recv_sem, device)
        copy.start()
        return copy

    def halo_copy(index, faces, diags, faces_in, diags_in, send_sem, recv_sem):
        dx, dy = AROUND[index]
        is_face, slot = face_slot(dx, dy)
        src = faces.at[slot] if is_face else diags.at[slot]
        dst = faces_in.at[slot] if is_face else diags_in.at[slot]
        return remote(src, dst, send_sem.at[index], recv_sem.at[index], at(dx, dy))

    def halo_start(*refs):
        for index, (dx, dy) in enumerate(AROUND):

            @pl.when(inside(dx, dy))
            def _():
                halo_copy(index, *refs).start()

    def halo_wait(*refs):
        for index, (dx, dy) in enumerate(AROUND):
            is_face, slot = face_slot(dx, dy)
            landed = refs[2] if is_face else refs[3]

            @pl.when(inside(-dx, -dy))
            def _():
                halo_copy(index, *refs).wait_recv()

            @pl.when(jnp.logical_not(inside(-dx, -dy)))
            def _():
                landed[slot] = jnp.zeros(landed.shape[1:], BF16)

            @pl.when(inside(dx, dy))
            def _():
                halo_copy(index, *refs).wait_send()

    pl.semaphore_wait(barrier, len(greeted))
    u_refs = (send_face, send_diag, halo_face, halo_diag, hu_send, hu_recv)
    wz_copy = push(w_pair.at[zhi], w_pair.at[zhi], wz_sem.at[0], wz_sem.at[1], partner)
    halo_start(*u_refs)
    loads[3].wait()
    take_in(g_ref, field_g, send_gface, send_gdiag)

    wz_copy.wait()
    w_parts[core, pos1, pos2] = w_pair[core]
    w_copies = []
    for k, device in enumerate(plane_peers):
        w_copies.append(
            push(
                w_pair.at[core], w_parts.at[core, pos1, pos2], wp_send.at[k], wp_recv.at[k], device
            )
        )

    halo_wait(*u_refs)
    g_refs = (send_gface, send_gdiag, halo_gface, halo_gdiag, hg_send, hg_recv)
    halo_start(*g_refs)

    def code_of(values, dx, dy):
        values = values.astype(F32)
        code = (values[0:1] + 8.0 * dx) * 1024.0 + (values[1:2] + 8.0 * dy) * 32.0 + values[2:3]
        return jnp.where(values[3:4] > 0.5, code, NOWHERE)

    codes = {(0, 0): code_of(meta, 0, 0)}
    for dx, dy in AROUND:
        is_face, slot = face_slot(-dx, -dy)
        codes[(dx, dy)] = code_of(halo_face[slot, 16] if is_face else halo_diag[slot, 4], dx, dy)
    own_place = (place[0:1] * 1024.0 + place[1:2] * 32.0 + place[2:3])[:, :NB]
    diagonal = iota((NB, NB), 0) == iota((NB, NB), 1)
    own_code = jnp.sum(jnp.where(diagonal, own_place, 0.0), axis=1, keepdims=True)

    picks = {}
    for ax in (-1, 0, 1):
        for ay in (-1, 0, 1):
            tiles = [(dx, dy) for dx in ((0, ax) if ax else (0,)) for dy in ((0, ay) if ay else (0,))]
            depth = NB * len(tiles)
            group = iota((1, depth), 1) // NB
            code_row = codes[tiles[0]][:, :depth]
            for n in range(1, len(tiles)):
                code_row = jnp.where(group == n, codes[tiles[n]][:, :depth], code_row)
            matches = []
            for oz in (-1, 0, 1):
                for ox, oy in tiles:
                    wanted = own_code + float(ox * 1024 + oy * 32 + oz)
                    matches.append(jnp.where(wanted == code_row, 1.0, 0.0))
            picks[(ax, ay)] = (tiles, jnp.concatenate(matches, axis=0).astype(BF16))

    def padded(cell, shift):
        return 0 if shift < 0 else (5 if shift > 0 else cell + 1)

    def assemble(field, faces, diags):
        def source(dx, dy, i, j, k):
            if dx == 0 and dy == 0:
                return field[i + 1, j + 1, k + 1]
            is_face, slot = face_slot(-dx, -dy)
            if not is_face:
                return diags[slot, k]
            return faces[slot, (j if dy == 0 else i) * 4 + k]

        for (ax, ay), (tiles, pick) in picks.items():
            count = len(tiles)
            for i in {-1: (3,), 0: (1, 2), 1: (0,)}[ax]:
                for j in {-1: (3,), 0: (1, 2), 1: (0,)}[ay]:
                    for k in range(4):
                        shifts = {0: (0, 1), 3: (-1, 0)}.get(k, (0,))
                        if count == 1 and k in (1, 2):
                            continue
                        first = (shifts[0] + 1) * count * NB
                        last = (shifts[-1] + 2) * count * NB
                        pool = [source(dx, dy, i, j, k) for dx, dy in tiles]
                        pool = pool[0] if count == 1 else jnp.concatenate(pool, axis=0)
                        got = exact_dot(pick[first:last], pool).astype(BF16)
                        row = 0
                        for oz in shifts:
                            for ox, oy in tiles:
                                if ox or oy or oz:
                                    to = padded(i, ox), padded(j, oy), padded(k, oz)
                                    field[to] = got[row : row + NB]
                                row += NB

    assemble(field_u, halo_face, halo_diag)

    def window(field, tap):
        a, b, e = tap // 9, tap // 3 % 3, tap % 3
        return field[a : a + 4, b : b + 4, e : e + 4].reshape(1024, CH)

    kept = field_g[1:5, 1:5, 1:5].reshape(1024, CH)
    dw_full[TAPS * CH :] = jnp.zeros((dw_full.shape[0] - TAPS * CH, CH), F32)

    def gradient(first, last):
        for tap in range(first, last):
            dw_full[tap * CH : (tap + 1) * CH] = lax.dot_general(
                window(field_u, tap), kept, (((0,), (0,)), ((), ())), preferred_element_type=F32
            )

    def split(which):
        for n in range(plane):
            for part in range(2):
                start = (which * plane + n) * rows + part * half
                nx, ny = n % side, n // side
                to = (nx, ny) if part == 0 else (ny, nx)
                dw_parts[part, which, to[0], to[1]] = dw_full[start : start + half_pad]
        return push(
            dw_parts.at[1 - core, which],
            swap_in.at[which],
            r0_send.at[which],
            r0_recv.at[which],
            sibling,
        )

    def phase_one(which, swap):
        swap.wait()
        chip_sum[which] = dw_parts[core, which] + swap_in[which]
        copies = []
        for k, device in enumerate(peers1):
            index = which * (side - 1) + k
            copies.append(
                push(
                    chip_sum.at[which, ones[k]],
                    one_in.at[which, k],
                    r1_send.at[index],
                    r1_recv.at[index],
                    device,
                )
            )
        return copies

    def phase_two(which, arriving):
        for copy in arriving:
            copy.wait()
        total = chip_sum[which, pos1]
        for k in range(side - 1):
            total = total + one_in[which, k]
        one_sum[which] = total
        copies = []
        for k, device in enumerate(peers2):
            index = which * (side - 1) + k
            copies.append(
                push(
                    one_sum.at[which, twos[k]],
                    two_in.at[which, k],
                    r2_send.at[index],
                    r2_recv.at[index],
                    device,
                )
            )
        return copies

    def phase_done(which, arriving):
        for copy in arriving:
            copy.wait()
        total = one_sum[which, pos2]
        for k in range(side - 1):
            total = total + two_in[which, k]
        plane_sum[which] = total

    gradient(0, 14)
    swap_low = split(0)
    gradient(14, TAPS)
    swap_high = split(1)
    one_low = phase_one(0, swap_low)
    one_high = phase_one(1, swap_high)
    for copy in w_copies:
        copy.wait()
    ws_copy = push(w_parts.at[core], w_parts.at[core], ws_sem.at[0], ws_sem.at[1], sibling)
    def convolve(field, weights, result_ref, i):
        total = None
        for tap in range(0, TAPS, 2):
            last = min(tap + 2, TAPS)
            left = []
            for n in range(tap, last):
                a, b, e = n // 9, n // 3 % 3, n % 3
                left.append(field[i + a, b : b + 4, e : e + 4].reshape(256, CH))
            left = left[0] if len(left) == 1 else jnp.concatenate(left, axis=1)
            term = exact_dot(left, weights[tap * CH : last * CH])
            total = term if total is None else total + term
        slab = exact_dot(turn_out, total.astype(BF16)).astype(BF16)
        result_ref[0, :, 16 * i : 16 * i + 16, :] = slab.reshape(NB, 16, CH)

    two_low = phase_two(0, one_low)
    two_high = phase_two(1, one_high)
    ws_copy.wait()
    for which in range(2):
        for n in range(plane):
            nx, ny = n % side, n // side
            to = (nx, ny) if which == 0 else (ny, nx)
            start = (which * plane + n) * rows
            w_full[start : start + rows] = w_parts[which, to[0], to[1], 0:rows]
    for tap in range(TAPS):
        w_turned[(26 - tap) * CH : (27 - tap) * CH] = w_full[tap * CH : (tap + 1) * CH].T

    for i in range(0, 2):
        convolve(field_u, w_full, out_ref, i)
    phase_done(0, two_low)
    phase_done(1, two_high)

    def piece_start(low):
        start = low * piece
        return pl.multiple_of(jnp.minimum(start, half_pad - piece), 8)

    z_copies = []
    for k, device in enumerate(z_peers):
        low = lax.rem(zeds[k], z_low)
        z_copies.append(
            push(
                plane_sum.at[zeds[k] // z_low, pl.ds(piece_start(low), piece)],
                z_in.at[k],
                r3_send.at[k],
                r3_recv.at[k],
                device,
            )
        )
    for i in range(2, 4):
        convolve(field_u, w_full, out_ref, i)
    halo_wait(*g_refs)
    assemble(field_g, halo_gface, halo_gdiag)
    for copy in z_copies:
        copy.wait()
    total = plane_sum[zhi, pl.ds(piece_start(zlo), piece)]
    for k in range(z_all - 1):
        total = total + z_in[k]
    pieces[p] = total * (1.0 / math.sqrt(gx_size * gy_size * NB * 64))
    last_copies = []
    for k, device in enumerate(gx_peers):
        last_copies.append(push(pieces.at[p], pieces.at[p], r4_send.at[k], r4_recv.at[k], device))
    for i in range(0, 4):
        convolve(field_g, w_turned, gf_ref, i)
    for copy in last_copies:
        copy.wait()
    for n in range(gx_size):
        part, low = n % 2, n // 2
        start = min(low * piece, half_pad - piece)
        count = min(piece, half - start)
        gw_ref[part * half + start : part * half + start + count] = pieces[n, 0:count]


def deliver(a_ref, b_ref, c_ref, a_out, b_out, c_out):
    a_out[...] = a_ref[...]
    b_out[...] = b_ref[...]
    c_out[...] = c_ref[...]


def hand_over(*arrays):
    return pl.pallas_call(
        deliver,
        out_shape=tuple(jax.ShapeDtypeStruct(a.shape, a.dtype) for a in arrays),
        in_specs=[pl.BlockSpec(memory_space=pltpu.VMEM)] * 3,
        out_specs=[pl.BlockSpec(memory_space=pltpu.VMEM)] * 3,
    )(*arrays)


def local(gx_size, gy_size, features, block_at, block_coords, weight, cotangent):
    plane = gy_size // 2
    side = math.isqrt(plane)
    z_low = gx_size // 2
    z_all = 2 * z_low
    rows = TAPS * CH // gy_size
    rows_pad = -(-rows // 16) * 16
    half_pad = -(-(rows // 2) // 8) * 8
    piece = -(-half_pad // (8 * z_low)) * 8
    blocks = pl.BlockSpec(memory_space=pltpu.VMEM)
    vmem = pltpu.VMEM
    dma = pltpu.SemaphoreType.DMA
    corners = block_coords.transpose(1, 0, 2)
    positions = block_at.reshape(-1, block_at.shape[2])
    results = pl.pallas_call(
        functools.partial(kernel, gx_size, gy_size, side),
        out_shape=(
            jax.ShapeDtypeStruct(features.shape, BF16),
            jax.ShapeDtypeStruct(features.shape, BF16),
            jax.ShapeDtypeStruct((rows, CH), F32),
        ),
        in_specs=[pl.BlockSpec(memory_space=pl.ANY)] * 5,
        out_specs=[blocks] * 3,
        scratch_shapes=[
            vmem(features.shape, BF16),
            vmem(positions.shape, jnp.int32),
            vmem(corners.shape, jnp.int32),
            vmem(weight.shape, BF16),
            vmem(features.shape, BF16),
            vmem((6, 6, 6, NB, CH), BF16),
            vmem((6, 6, 6, NB, CH), BF16),
            vmem((4, 17, NB, CH), BF16),
            vmem((4, 5, NB, CH), BF16),
            vmem((4, 17, NB, CH), BF16),
            vmem((4, 5, NB, CH), BF16),
            vmem((4, 16, NB, CH), BF16),
            vmem((4, 4, NB, CH), BF16),
            vmem((4, 16, NB, CH), BF16),
            vmem((4, 4, NB, CH), BF16),
            vmem((2, rows_pad, CH), BF16),
            vmem((2, side, side, rows_pad, CH), BF16),
            vmem((TAPS * CH, CH), BF16),
            vmem((TAPS * CH, CH), BF16),
            vmem((TAPS * CH + 16, CH), F32),
            vmem((2, 2, side, side, half_pad, CH), F32),
            vmem((2, side, side, half_pad, CH), F32),
            vmem((2, side, side, half_pad, CH), F32),
            vmem((2, side - 1, side, half_pad, CH), F32),
            vmem((2, side, half_pad, CH), F32),
            vmem((2, side - 1, half_pad, CH), F32),
            vmem((2, half_pad, CH), F32),
            vmem((z_all - 1, piece, CH), F32),
            vmem((gx_size, piece, CH), F32),
            dma((5,)),
            dma((8,)),
            dma((8,)),
            dma((8,)),
            dma((8,)),
            dma((2,)),
            dma((plane - 1,)),
            dma((plane - 1,)),
            dma((2,)),
            dma((2,)),
            dma((2,)),
            dma((2 * side - 2,)),
            dma((2 * side - 2,)),
            dma((2 * side - 2,)),
            dma((2 * side - 2,)),
            dma((z_all - 1,)),
            dma((z_all - 1,)),
            dma((gx_size - 1,)),
            dma((gx_size - 1,)),
        ],
        compiler_params=pltpu.CompilerParams(
            collective_id=0, has_side_effects=True, vmem_limit_bytes=63 * 1024 * 1024
        ),
    )(features, positions, corners, weight, cotangent)
    return hand_over(*results)


def solution(mesh):
    placed = (
        P("gx", "gy", None, None),
        P("gx", "gy", None),
        P("gx", None, "gy"),
        P("gy", None),
        P("gx", "gy", None, None),
    )
    return jax.shard_map(
        functools.partial(local, mesh.shape["gx"], mesh.shape["gy"]),
        mesh=mesh,
        in_specs=placed,
        out_specs=(P("gx", "gy", None, None), P("gx", "gy", None, None), P("gy", None)),
        check_vma=False,
    )
```

```python
import functools
import math

import jax
import jax.numpy as jnp
from jax import lax
from jax.experimental import pallas as pl
from jax.experimental.pallas import tpu as pltpu
from jax.sharding import PartitionSpec as P

MESH = pl.DeviceIdType.MESH
F32 = jnp.float32
BF16 = jnp.bfloat16
CH = 128
NB = 16
TAPS = 27
NOWHERE = -1.0e6
AROUND = [(dx, dy) for dx in (-1, 0, 1) for dy in (-1, 0, 1) if dx or dy]


def iota(shape, dim):
    return lax.broadcasted_iota(jnp.int32, shape, dim)


def zero_one(mask):
    return jnp.where(mask, 1.0, 0.0).astype(BF16)


def exact_dot(left, right):
    return jnp.dot(left, right, preferred_element_type=F32)


def face_slot(dx, dy):
    if dy == 0:
        return True, 0 if dx > 0 else 1
    if dx == 0:
        return True, 2 if dy > 0 else 3
    return False, (0 if dx > 0 else 2) + (0 if dy > 0 else 1)


def kernel(
    gx_size,
    gy_size,
    side,
    f_hbm,
    at_hbm,
    coords_hbm,
    w_hbm,
    g_hbm,
    out_ref,
    gf_ref,
    gw_ref,
    f_ref,
    at_ref,
    coords_ref,
    w_ref,
    g_ref,
    field_u,
    field_g,
    send_face,
    send_diag,
    halo_face,
    halo_diag,
    send_gface,
    send_gdiag,
    halo_gface,
    halo_gdiag,
    w_pair,
    w_parts,
    w_full,
    w_turned,
    dw_full,
    dw_parts,
    swap_in,
    chip_sum,
    one_in,
    one_sum,
    two_in,
    plane_sum,
    z_in,
    pieces,
    in_sem,
    hu_send,
    hu_recv,
    hg_send,
    hg_recv,
    wz_sem,
    wp_send,
    wp_recv,
    ws_sem,
    r0_send,
    r0_recv,
    r1_send,
    r1_recv,
    r2_send,
    r2_recv,
    r3_send,
    r3_recv,
    r4_send,
    r4_recv,
):
    plane = side * side
    z_low = gx_size // 2
    z_all = 2 * z_low
    rows = TAPS * CH // gy_size
    half = rows // 2
    half_pad = plane_sum.shape[1]
    piece = pieces.shape[1]
    p = lax.axis_index("gx")
    q = lax.axis_index("gy")
    core = lax.rem(p, 2)
    zlo = p // 2
    zhi = q // plane
    spot = lax.rem(q, plane)
    zed = zhi * z_low + zlo
    x = lax.rem(spot, side)
    y = spot // side
    pos1 = x + core * (y - x)
    pos2 = y + core * (x - y)
    step1 = 1 + core * (side - 1)
    step2 = side - core * (side - 1)

    sibling = (p + 1 - 2 * core, q)
    partner = (p, spot + (1 - zhi) * plane)
    ones = [lax.rem(pos1 + k, side) for k in range(1, side)]
    twos = [lax.rem(pos2 + k, side) for k in range(1, side)]
    peers1 = [(p, zhi * plane + n * step1 + pos2 * step2) for n in ones]
    peers2 = [(p, zhi * plane + pos1 * step1 + n * step2) for n in twos]
    plane_peers = []
    for k in range(1, plane):
        n1, n2 = lax.rem(pos1 + k % side, side), lax.rem(pos2 + k // side, side)
        plane_peers.append((p, zhi * plane + n1 * step1 + n2 * step2))
    zeds = [lax.rem(zed + k, z_all) for k in range(1, z_all)]
    z_peers = [(lax.rem(z, z_low) * 2 + core, (z // z_low) * plane + spot) for z in zeds]
    gx_peers = [(lax.rem(p + k, gx_size), q) for k in range(1, gx_size)]

    def at(dx, dy):
        return (lax.rem(p + dx + gx_size, gx_size), lax.rem(q + dy + gy_size, gy_size))

    def inside(dx, dy):
        return (p + dx >= 0) & (p + dx < gx_size) & (q + dy >= 0) & (q + dy < gy_size)

    barrier = pltpu.get_barrier_semaphore()
    greeted = [sibling, partner] + plane_peers + z_peers + gx_peers
    greeted = greeted + [at(dx, dy) for dx, dy in AROUND]
    for device in greeted:
        pl.semaphore_signal(barrier, inc=1, device_id=device, device_id_type=MESH)
    loads = []
    pairs = ((at_hbm, at_ref), (coords_hbm, coords_ref), (f_hbm, f_ref), (g_hbm, g_ref), (w_hbm, w_ref))
    for index, (src, dst) in enumerate(pairs):
        copy = pltpu.make_async_copy(src, dst, in_sem.at[index])
        copy.start()
        loads.append(copy)

    loads[0].wait()
    loads[1].wait()
    lane_slot = lax.rem(iota((1, CH), 1), NB).astype(F32)
    found = jnp.zeros((at_ref.shape[0], CH), F32)
    placed = at_ref[...].astype(F32)
    for z in range(placed.shape[1]):
        found = jnp.maximum(found, jnp.where(placed[:, z : z + 1] == lane_slot, 1.0, 0.0))
    live = jnp.max(found, axis=0, keepdims=True)
    spread = zero_one(lax.rem(iota((NB, CH), 1), NB) == iota((NB, CH), 0))
    coords = coords_ref[:, 0, :].astype(F32).astype(BF16)
    place = exact_dot(coords, spread)
    meta = jnp.concatenate([place, live, jnp.zeros((NB - 4, CH), F32)], axis=0).astype(BF16)

    live_rows = jnp.broadcast_to(live[:, :NB], (8, NB)).astype(BF16)
    by_high = zero_one(iota((NB, NB * NB), 1) // NB == iota((NB, NB * NB), 0))
    by_low = zero_one(lax.rem(iota((NB, NB * NB), 1), NB) == iota((NB, NB * NB), 0))
    live_high = exact_dot(live_rows, by_high)[0:1]
    live_low = exact_dot(live_rows, by_low)[0:1]
    row_id = iota((NB * NB, NB * NB), 0)
    col_id = iota((NB * NB, NB * NB), 1)
    turned = (lax.rem(row_id, NB) == col_id // NB) & (row_id // NB == lax.rem(col_id, NB))
    turn = jnp.where(turned, 1.0, 0.0)
    turn_in = (turn * live_high).astype(BF16)
    turn_out = (turn * live_low).astype(BF16)

    def take_in(ref, field, faces, diags):
        for i in range(4):
            block = ref[0, :, 16 * i : 16 * i + 16, :].reshape(NB * NB, CH)
            slab = exact_dot(turn_in, block).astype(BF16).reshape(4, 4, NB, CH)
            field[i + 1, 1:5, 1:5] = slab
            for which, along in ((0, 3), (1, 0)):
                if i == along:
                    faces[which, 0:16] = slab.reshape(16, NB, CH)
                    diags[2 * which, 0:4] = slab[3]
                    diags[2 * which + 1, 0:4] = slab[0]
            faces[2, 4 * i : 4 * i + 4] = slab[3]
            faces[3, 4 * i : 4 * i + 4] = slab[0]

    loads[2].wait()
    take_in(f_ref, field_u, send_face, send_diag)
    for n in range(4):
        send_face[n, 16] = meta
        send_diag[n, 4] = meta
    loads[4].wait()
    w_pair[zhi] = jnp.zeros((w_pair.shape[1], CH), BF16)
    w_pair[zhi, 0:rows] = w_ref[...]

    def remote(src, dst, send_sem, recv_sem, device):
        return pltpu.make_async_remote_copy(
            src_ref=src,
            dst_ref=dst,
            send_sem=send_sem,
            recv_sem=recv_sem,
            device_id=device,
            device_id_type=MESH,
        )

    def push(src, dst, send_sem, recv_sem, device):
        copy = remote(src, dst, send_sem, recv_sem, device)
        copy.start()
        return copy

    def halo_copy(index, faces, diags, faces_in, diags_in, send_sem, recv_sem):
        dx, dy = AROUND[index]
        is_face, slot = face_slot(dx, dy)
        src = faces.at[slot] if is_face else diags.at[slot]
        dst = faces_in.at[slot] if is_face else diags_in.at[slot]
        return remote(src, dst, send_sem.at[index], recv_sem.at[index], at(dx, dy))

    def halo_start(*refs):
        for index, (dx, dy) in enumerate(AROUND):

            @pl.when(inside(dx, dy))
            def _():
                halo_copy(index, *refs).start()

    def halo_wait(*refs):
        for index, (dx, dy) in enumerate(AROUND):
            is_face, slot = face_slot(dx, dy)
            landed = refs[2] if is_face else refs[3]

            @pl.when(inside(-dx, -dy))
            def _():
                halo_copy(index, *refs).wait_recv()

            @pl.when(jnp.logical_not(inside(-dx, -dy)))
            def _():
                landed[slot] = jnp.zeros(landed.shape[1:], BF16)

            @pl.when(inside(dx, dy))
            def _():
                halo_copy(index, *refs).wait_send()

    pl.semaphore_wait(barrier, len(greeted))
    u_refs = (send_face, send_diag, halo_face, halo_diag, hu_send, hu_recv)
    wz_copy = push(w_pair.at[zhi], w_pair.at[zhi], wz_sem.at[0], wz_sem.at[1], partner)
    halo_start(*u_refs)
    loads[3].wait()
    take_in(g_ref, field_g, send_gface, send_gdiag)

    wz_copy.wait()
    w_parts[core, pos1, pos2] = w_pair[core]
    w_copies = []
    for k, device in enumerate(plane_peers):
        w_copies.append(
            push(
                w_pair.at[core], w_parts.at[core, pos1, pos2], wp_send.at[k], wp_recv.at[k], device
            )
        )

    halo_wait(*u_refs)
    g_refs = (send_gface, send_gdiag, halo_gface, halo_gdiag, hg_send, hg_recv)
    halo_start(*g_refs)

    def code_of(values, dx, dy):
        values = values.astype(F32)
        code = (values[0:1] + 8.0 * dx) * 1024.0 + (values[1:2] + 8.0 * dy) * 32.0 + values[2:3]
        return jnp.where(values[3:4] > 0.5, code, NOWHERE)

    codes = {(0, 0): code_of(meta, 0, 0)}
    for dx, dy in AROUND:
        is_face, slot = face_slot(-dx, -dy)
        codes[(dx, dy)] = code_of(halo_face[slot, 16] if is_face else halo_diag[slot, 4], dx, dy)
    own_place = (place[0:1] * 1024.0 + place[1:2] * 32.0 + place[2:3])[:, :NB]
    diagonal = iota((NB, NB), 0) == iota((NB, NB), 1)
    own_code = jnp.sum(jnp.where(diagonal, own_place, 0.0), axis=1, keepdims=True)

    picks = {}
    for ax in (-1, 0, 1):
        for ay in (-1, 0, 1):
            tiles = [(dx, dy) for dx in ((0, ax) if ax else (0,)) for dy in ((0, ay) if ay else (0,))]
            depth = NB * len(tiles)
            group = iota((1, depth), 1) // NB
            code_row = codes[tiles[0]][:, :depth]
            for n in range(1, len(tiles)):
                code_row = jnp.where(group == n, codes[tiles[n]][:, :depth], code_row)
            matches = []
            for oz in (-1, 0, 1):
                for ox, oy in tiles:
                    wanted = own_code + float(ox * 1024 + oy * 32 + oz)
                    matches.append(jnp.where(wanted == code_row, 1.0, 0.0))
            picks[(ax, ay)] = (tiles, jnp.concatenate(matches, axis=0).astype(BF16))

    def padded(cell, shift):
        return 0 if shift < 0 else (5 if shift > 0 else cell + 1)

    def assemble(field, faces, diags):
        def source(dx, dy, i, j, k):
            if dx == 0 and dy == 0:
                return field[i + 1, j + 1, k + 1]
            is_face, slot = face_slot(-dx, -dy)
            if not is_face:
                return diags[slot, k]
            return faces[slot, (j if dy == 0 else i) * 4 + k]

        for (ax, ay), (tiles, pick) in picks.items():
            count = len(tiles)
            for i in {-1: (3,), 0: (1, 2), 1: (0,)}[ax]:
                for j in {-1: (3,), 0: (1, 2), 1: (0,)}[ay]:
                    for k in range(4):
                        shifts = {0: (0, 1), 3: (-1, 0)}.get(k, (0,))
                        if count == 1 and k in (1, 2):
                            continue
                        first = (shifts[0] + 1) * count * NB
                        last = (shifts[-1] + 2) * count * NB
                        pool = [source(dx, dy, i, j, k) for dx, dy in tiles]
                        pool = pool[0] if count == 1 else jnp.concatenate(pool, axis=0)
                        got = exact_dot(pick[first:last], pool).astype(BF16)
                        row = 0
                        for oz in shifts:
                            for ox, oy in tiles:
                                if ox or oy or oz:
                                    to = padded(i, ox), padded(j, oy), padded(k, oz)
                                    field[to] = got[row : row + NB]
                                row += NB

    assemble(field_u, halo_face, halo_diag)

    def window(field, tap):
        a, b, e = tap // 9, tap // 3 % 3, tap % 3
        return field[a : a + 4, b : b + 4, e : e + 4].reshape(1024, CH)

    kept_turned = field_g[1:5, 1:5, 1:5].reshape(1024, CH).T
    dw_full[TAPS * CH :] = jnp.zeros((dw_full.shape[0] - TAPS * CH, CH), F32)

    def gradient(first, last):
        for tap in range(first, last, 2):
            upto = min(tap + 2, last)
            right = [window(field_u, n) for n in range(tap, upto)]
            right = right[0] if len(right) == 1 else jnp.concatenate(right, axis=1)
            dw_full[tap * CH : upto * CH] = exact_dot(kept_turned, right).T

    def split(which):
        for n in range(plane):
            for part in range(2):
                start = (which * plane + n) * rows + part * half
                nx, ny = n % side, n // side
                to = (nx, ny) if part == 0 else (ny, nx)
                dw_parts[part, which, to[0], to[1]] = dw_full[start : start + half_pad]
        return push(
            dw_parts.at[1 - core, which],
            swap_in.at[which],
            r0_send.at[which],
            r0_recv.at[which],
            sibling,
        )

    def phase_one(which, swap):
        swap.wait()
        chip_sum[which] = dw_parts[core, which] + swap_in[which]
        copies = []
        for k, device in enumerate(peers1):
            index = which * (side - 1) + k
            copies.append(
                push(
                    chip_sum.at[which, ones[k]],
                    one_in.at[which, k],
                    r1_send.at[index],
                    r1_recv.at[index],
                    device,
                )
            )
        return copies

    def phase_two(which, arriving):
        for copy in arriving:
            copy.wait()
        total = chip_sum[which, pos1]
        for k in range(side - 1):
            total = total + one_in[which, k]
        one_sum[which] = total
        copies = []
        for k, device in enumerate(peers2):
            index = which * (side - 1) + k
            copies.append(
                push(
                    one_sum.at[which, twos[k]],
                    two_in.at[which, k],
                    r2_send.at[index],
                    r2_recv.at[index],
                    device,
                )
            )
        return copies

    def phase_done(which, arriving):
        for copy in arriving:
            copy.wait()
        total = one_sum[which, pos2]
        for k in range(side - 1):
            total = total + two_in[which, k]
        plane_sum[which] = total

    gradient(0, 14)
    swap_low = split(0)
    gradient(14, TAPS)
    swap_high = split(1)
    one_low = phase_one(0, swap_low)
    one_high = phase_one(1, swap_high)
    for copy in w_copies:
        copy.wait()
    ws_copy = push(w_parts.at[core], w_parts.at[core], ws_sem.at[0], ws_sem.at[1], sibling)
    def convolve(field, weights, result_ref, i):
        total = None
        for tap in range(0, TAPS, 2):
            last = min(tap + 2, TAPS)
            left = []
            for n in range(tap, last):
                a, b, e = n // 9, n // 3 % 3, n % 3
                left.append(field[i + a, b : b + 4, e : e + 4].reshape(256, CH))
            left = left[0] if len(left) == 1 else jnp.concatenate(left, axis=1)
            term = exact_dot(left, weights[tap * CH : last * CH])
            total = term if total is None else total + term
        slab = exact_dot(turn_out, total.astype(BF16)).astype(BF16)
        result_ref[0, :, 16 * i : 16 * i + 16, :] = slab.reshape(NB, 16, CH)

    two_low = phase_two(0, one_low)
    two_high = phase_two(1, one_high)
    ws_copy.wait()
    for which in range(2):
        for n in range(plane):
            nx, ny = n % side, n // side
            to = (nx, ny) if which == 0 else (ny, nx)
            start = (which * plane + n) * rows
            w_full[start : start + rows] = w_parts[which, to[0], to[1], 0:rows]
    for tap in range(TAPS):
        w_turned[(26 - tap) * CH : (27 - tap) * CH] = w_full[tap * CH : (tap + 1) * CH].T

    for i in range(0, 2):
        convolve(field_u, w_full, out_ref, i)
    phase_done(0, two_low)
    phase_done(1, two_high)

    def piece_start(low):
        start = low * piece
        return pl.multiple_of(jnp.minimum(start, half_pad - piece), 8)

    z_copies = []
    for k, device in enumerate(z_peers):
        low = lax.rem(zeds[k], z_low)
        z_copies.append(
            push(
                plane_sum.at[zeds[k] // z_low, pl.ds(piece_start(low), piece)],
                z_in.at[k],
                r3_send.at[k],
                r3_recv.at[k],
                device,
            )
        )
    for i in range(2, 4):
        convolve(field_u, w_full, out_ref, i)
    halo_wait(*g_refs)
    assemble(field_g, halo_gface, halo_gdiag)
    for copy in z_copies:
        copy.wait()
    total = plane_sum[zhi, pl.ds(piece_start(zlo), piece)]
    for k in range(z_all - 1):
        total = total + z_in[k]
    pieces[p] = total * (1.0 / math.sqrt(gx_size * gy_size * NB * 64))
    last_copies = []
    for k, device in enumerate(gx_peers):
        last_copies.append(push(pieces.at[p], pieces.at[p], r4_send.at[k], r4_recv.at[k], device))
    for i in range(0, 4):
        convolve(field_g, w_turned, gf_ref, i)
    for copy in last_copies:
        copy.wait()
    for n in range(gx_size):
        part, low = n % 2, n // 2
        start = min(low * piece, half_pad - piece)
        count = min(piece, half - start)
        gw_ref[part * half + start : part * half + start + count] = pieces[n, 0:count]


def deliver(a_ref, b_ref, c_ref, a_out, b_out, c_out):
    a_out[...] = a_ref[...]
    b_out[...] = b_ref[...]
    c_out[...] = c_ref[...]


def hand_over(*arrays):
    return pl.pallas_call(
        deliver,
        out_shape=tuple(jax.ShapeDtypeStruct(a.shape, a.dtype) for a in arrays),
        in_specs=[pl.BlockSpec(memory_space=pltpu.VMEM)] * 3,
        out_specs=[pl.BlockSpec(memory_space=pltpu.VMEM)] * 3,
    )(*arrays)


def local(gx_size, gy_size, features, block_at, block_coords, weight, cotangent):
    plane = gy_size // 2
    side = math.isqrt(plane)
    z_low = gx_size // 2
    z_all = 2 * z_low
    rows = TAPS * CH // gy_size
    rows_pad = -(-rows // 16) * 16
    half_pad = -(-(rows // 2) // 8) * 8
    piece = -(-half_pad // (8 * z_low)) * 8
    blocks = pl.BlockSpec(memory_space=pltpu.VMEM)
    vmem = pltpu.VMEM
    dma = pltpu.SemaphoreType.DMA
    corners = block_coords.transpose(1, 0, 2)
    positions = block_at.reshape(-1, block_at.shape[2])
    results = pl.pallas_call(
        functools.partial(kernel, gx_size, gy_size, side),
        out_shape=(
            jax.ShapeDtypeStruct(features.shape, BF16),
            jax.ShapeDtypeStruct(features.shape, BF16),
            jax.ShapeDtypeStruct((rows, CH), F32),
        ),
        in_specs=[pl.BlockSpec(memory_space=pl.ANY)] * 5,
        out_specs=[blocks] * 3,
        scratch_shapes=[
            vmem(features.shape, BF16),
            vmem(positions.shape, jnp.int32),
            vmem(corners.shape, jnp.int32),
            vmem(weight.shape, BF16),
            vmem(features.shape, BF16),
            vmem((6, 6, 6, NB, CH), BF16),
            vmem((6, 6, 6, NB, CH), BF16),
            vmem((4, 17, NB, CH), BF16),
            vmem((4, 5, NB, CH), BF16),
            vmem((4, 17, NB, CH), BF16),
            vmem((4, 5, NB, CH), BF16),
            vmem((4, 16, NB, CH), BF16),
            vmem((4, 4, NB, CH), BF16),
            vmem((4, 16, NB, CH), BF16),
            vmem((4, 4, NB, CH), BF16),
            vmem((2, rows_pad, CH), BF16),
            vmem((2, side, side, rows_pad, CH), BF16),
            vmem((TAPS * CH, CH), BF16),
            vmem((TAPS * CH, CH), BF16),
            vmem((TAPS * CH + 16, CH), F32),
            vmem((2, 2, side, side, half_pad, CH), F32),
            vmem((2, side, side, half_pad, CH), F32),
            vmem((2, side, side, half_pad, CH), F32),
            vmem((2, side - 1, side, half_pad, CH), F32),
            vmem((2, side, half_pad, CH), F32),
            vmem((2, side - 1, half_pad, CH), F32),
            vmem((2, half_pad, CH), F32),
            vmem((z_all - 1, piece, CH), F32),
            vmem((gx_size, piece, CH), F32),
            dma((5,)),
            dma((8,)),
            dma((8,)),
            dma((8,)),
            dma((8,)),
            dma((2,)),
            dma((plane - 1,)),
            dma((plane - 1,)),
            dma((2,)),
            dma((2,)),
            dma((2,)),
            dma((2 * side - 2,)),
            dma((2 * side - 2,)),
            dma((2 * side - 2,)),
            dma((2 * side - 2,)),
            dma((z_all - 1,)),
            dma((z_all - 1,)),
            dma((gx_size - 1,)),
            dma((gx_size - 1,)),
        ],
        compiler_params=pltpu.CompilerParams(
            collective_id=0, has_side_effects=True, vmem_limit_bytes=63 * 1024 * 1024
        ),
    )(features, positions, corners, weight, cotangent)
    return hand_over(*results)


def solution(mesh):
    placed = (
        P("gx", "gy", None, None),
        P("gx", "gy", None),
        P("gx", None, "gy"),
        P("gy", None),
        P("gx", "gy", None, None),
    )
    return jax.shard_map(
        functools.partial(local, mesh.shape["gx"], mesh.shape["gy"]),
        mesh=mesh,
        in_specs=placed,
        out_specs=(P("gx", "gy", None, None), P("gx", "gy", None, None), P("gy", None)),
        check_vma=False,
    )
```

```python
import functools
import math

import jax
import jax.numpy as jnp
from jax import lax
from jax.experimental import pallas as pl
from jax.experimental.pallas import tpu as pltpu
from jax.sharding import PartitionSpec as P

MESH = pl.DeviceIdType.MESH
F32 = jnp.float32
BF16 = jnp.bfloat16
CH = 128
NB = 16
TAPS = 27
NOWHERE = -1.0e6
AROUND = [(dx, dy) for dx in (-1, 0, 1) for dy in (-1, 0, 1) if dx or dy]


def iota(shape, dim):
    return lax.broadcasted_iota(jnp.int32, shape, dim)


def zero_one(mask):
    return jnp.where(mask, 1.0, 0.0).astype(BF16)


def exact_dot(left, right):
    return jnp.dot(left, right, preferred_element_type=F32)


def face_slot(dx, dy):
    if dy == 0:
        return True, 0 if dx > 0 else 1
    if dx == 0:
        return True, 2 if dy > 0 else 3
    return False, (0 if dx > 0 else 2) + (0 if dy > 0 else 1)


def kernel(
    gx_size,
    gy_size,
    side,
    f_hbm,
    at_hbm,
    coords_hbm,
    w_hbm,
    g_hbm,
    out_ref,
    gf_ref,
    gw_ref,
    f_ref,
    at_ref,
    coords_ref,
    w_ref,
    g_ref,
    field_u,
    field_g,
    send_face,
    send_diag,
    halo_face,
    halo_diag,
    send_gface,
    send_gdiag,
    halo_gface,
    halo_gdiag,
    w_pair,
    w_parts,
    w_full,
    w_turned,
    dw_full,
    dw_parts,
    swap_in,
    chip_sum,
    one_in,
    one_sum,
    two_in,
    plane_sum,
    z_in,
    pieces,
    in_sem,
    hu_send,
    hu_recv,
    hg_send,
    hg_recv,
    wz_sem,
    wp_send,
    wp_recv,
    ws_sem,
    r0_send,
    r0_recv,
    r1_send,
    r1_recv,
    r2_send,
    r2_recv,
    r3_send,
    r3_recv,
    r4_send,
    r4_recv,
):
    plane = side * side
    z_low = gx_size // 2
    z_all = 2 * z_low
    rows = TAPS * CH // gy_size
    half = rows // 2
    half_pad = plane_sum.shape[1]
    piece = pieces.shape[1]
    p = lax.axis_index("gx")
    q = lax.axis_index("gy")
    core = lax.rem(p, 2)
    zlo = p // 2
    zhi = q // plane
    spot = lax.rem(q, plane)
    zed = zhi * z_low + zlo
    x = lax.rem(spot, side)
    y = spot // side
    pos1 = x + core * (y - x)
    pos2 = y + core * (x - y)
    step1 = 1 + core * (side - 1)
    step2 = side - core * (side - 1)

    sibling = (p + 1 - 2 * core, q)
    partner = (p, spot + (1 - zhi) * plane)
    ones = [lax.rem(pos1 + k, side) for k in range(1, side)]
    twos = [lax.rem(pos2 + k, side) for k in range(1, side)]
    peers1 = [(p, zhi * plane + n * step1 + pos2 * step2) for n in ones]
    peers2 = [(p, zhi * plane + pos1 * step1 + n * step2) for n in twos]
    plane_peers = []
    for k in range(1, plane):
        n1, n2 = lax.rem(pos1 + k % side, side), lax.rem(pos2 + k // side, side)
        plane_peers.append((p, zhi * plane + n1 * step1 + n2 * step2))
    zeds = [lax.rem(zed + k, z_all) for k in range(1, z_all)]
    z_peers = [(lax.rem(z, z_low) * 2 + core, (z // z_low) * plane + spot) for z in zeds]
    gx_peers = [(lax.rem(p + k, gx_size), q) for k in range(1, gx_size)]

    def at(dx, dy):
        return (lax.rem(p + dx + gx_size, gx_size), lax.rem(q + dy + gy_size, gy_size))

    def inside(dx, dy):
        return (p + dx >= 0) & (p + dx < gx_size) & (q + dy >= 0) & (q + dy < gy_size)

    barrier = pltpu.get_barrier_semaphore()
    greeted = [sibling, partner] + plane_peers + z_peers + gx_peers
    greeted = greeted + [at(dx, dy) for dx, dy in AROUND]
    for device in greeted:
        pl.semaphore_signal(barrier, inc=1, device_id=device, device_id_type=MESH)
    loads = []
    pairs = ((at_hbm, at_ref), (coords_hbm, coords_ref), (f_hbm, f_ref), (g_hbm, g_ref), (w_hbm, w_ref))
    for index, (src, dst) in enumerate(pairs):
        copy = pltpu.make_async_copy(src, dst, in_sem.at[index])
        copy.start()
        loads.append(copy)

    loads[0].wait()
    loads[1].wait()
    lane_slot = lax.rem(iota((1, CH), 1), NB).astype(F32)
    found = jnp.zeros((at_ref.shape[0], CH), F32)
    placed = at_ref[...].astype(F32)
    for z in range(placed.shape[1]):
        found = jnp.maximum(found, jnp.where(placed[:, z : z + 1] == lane_slot, 1.0, 0.0))
    live = jnp.max(found, axis=0, keepdims=True)
    spread = zero_one(lax.rem(iota((NB, CH), 1), NB) == iota((NB, CH), 0))
    coords = coords_ref[:, 0, :].astype(F32).astype(BF16)
    place = exact_dot(coords, spread)
    meta = jnp.concatenate([place, live, jnp.zeros((NB - 4, CH), F32)], axis=0).astype(BF16)

    live_rows = jnp.broadcast_to(live[:, :NB], (8, NB)).astype(BF16)
    by_high = zero_one(iota((NB, NB * NB), 1) // NB == iota((NB, NB * NB), 0))
    by_low = zero_one(lax.rem(iota((NB, NB * NB), 1), NB) == iota((NB, NB * NB), 0))
    live_high = exact_dot(live_rows, by_high)[0:1]
    live_low = exact_dot(live_rows, by_low)[0:1]
    row_id = iota((NB * NB, NB * NB), 0)
    col_id = iota((NB * NB, NB * NB), 1)
    turned = (lax.rem(row_id, NB) == col_id // NB) & (row_id // NB == lax.rem(col_id, NB))
    turn = jnp.where(turned, 1.0, 0.0)
    turn_in = (turn * live_high).astype(BF16)
    turn_out = (turn * live_low).astype(BF16)

    def take_in(ref, field, faces, diags):
        for i in range(4):
            block = ref[0, :, 16 * i : 16 * i + 16, :].reshape(NB * NB, CH)
            slab = exact_dot(turn_in, block).astype(BF16).reshape(4, 4, NB, CH)
            field[i + 1, 1:5, 1:5] = slab
            for which, along in ((0, 3), (1, 0)):
                if i == along:
                    faces[which, 0:16] = slab.reshape(16, NB, CH)
                    diags[2 * which, 0:4] = slab[3]
                    diags[2 * which + 1, 0:4] = slab[0]
            faces[2, 4 * i : 4 * i + 4] = slab[3]
            faces[3, 4 * i : 4 * i + 4] = slab[0]

    loads[2].wait()
    take_in(f_ref, field_u, send_face, send_diag)
    for n in range(4):
        send_face[n, 16] = meta
        send_diag[n, 4] = meta
    loads[4].wait()
    w_pair[zhi] = jnp.zeros((w_pair.shape[1], CH), BF16)
    w_pair[zhi, 0:rows] = w_ref[...]

    def remote(src, dst, send_sem, recv_sem, device):
        return pltpu.make_async_remote_copy(
            src_ref=src,
            dst_ref=dst,
            send_sem=send_sem,
            recv_sem=recv_sem,
            device_id=device,
            device_id_type=MESH,
        )

    def push(src, dst, send_sem, recv_sem, device):
        copy = remote(src, dst, send_sem, recv_sem, device)
        copy.start()
        return copy

    def halo_copy(index, faces, diags, faces_in, diags_in, send_sem, recv_sem):
        dx, dy = AROUND[index]
        is_face, slot = face_slot(dx, dy)
        src = faces.at[slot] if is_face else diags.at[slot]
        dst = faces_in.at[slot] if is_face else diags_in.at[slot]
        return remote(src, dst, send_sem.at[index], recv_sem.at[index], at(dx, dy))

    def halo_start(*refs):
        for index, (dx, dy) in enumerate(AROUND):

            @pl.when(inside(dx, dy))
            def _():
                halo_copy(index, *refs).start()

    def halo_wait(*refs):
        for index, (dx, dy) in enumerate(AROUND):
            is_face, slot = face_slot(dx, dy)
            landed = refs[2] if is_face else refs[3]

            @pl.when(inside(-dx, -dy))
            def _():
                halo_copy(index, *refs).wait_recv()

            @pl.when(jnp.logical_not(inside(-dx, -dy)))
            def _():
                landed[slot] = jnp.zeros(landed.shape[1:], BF16)

            @pl.when(inside(dx, dy))
            def _():
                halo_copy(index, *refs).wait_send()

    pl.semaphore_wait(barrier, len(greeted))
    u_refs = (send_face, send_diag, halo_face, halo_diag, hu_send, hu_recv)
    wz_copy = push(w_pair.at[zhi], w_pair.at[zhi], wz_sem.at[0], wz_sem.at[1], partner)
    halo_start(*u_refs)
    loads[3].wait()
    take_in(g_ref, field_g, send_gface, send_gdiag)

    wz_copy.wait()
    w_parts[core, pos1, pos2] = w_pair[core]
    w_copies = []
    for k, device in enumerate(plane_peers):
        w_copies.append(
            push(
                w_pair.at[core], w_parts.at[core, pos1, pos2], wp_send.at[k], wp_recv.at[k], device
            )
        )

    halo_wait(*u_refs)
    g_refs = (send_gface, send_gdiag, halo_gface, halo_gdiag, hg_send, hg_recv)
    halo_start(*g_refs)

    def code_of(values, dx, dy):
        values = values.astype(F32)
        code = (values[0:1] + 8.0 * dx) * 1024.0 + (values[1:2] + 8.0 * dy) * 32.0 + values[2:3]
        return jnp.where(values[3:4] > 0.5, code, NOWHERE)

    codes = {(0, 0): code_of(meta, 0, 0)}
    for dx, dy in AROUND:
        is_face, slot = face_slot(-dx, -dy)
        codes[(dx, dy)] = code_of(halo_face[slot, 16] if is_face else halo_diag[slot, 4], dx, dy)
    own_place = (place[0:1] * 1024.0 + place[1:2] * 32.0 + place[2:3])[:, :NB]
    diagonal = iota((NB, NB), 0) == iota((NB, NB), 1)
    own_code = jnp.sum(jnp.where(diagonal, own_place, 0.0), axis=1, keepdims=True)

    picks = {}
    for ax in (-1, 0, 1):
        for ay in (-1, 0, 1):
            tiles = [(dx, dy) for dx in ((0, ax) if ax else (0,)) for dy in ((0, ay) if ay else (0,))]
            depth = NB * len(tiles)
            group = iota((1, depth), 1) // NB
            code_row = codes[tiles[0]][:, :depth]
            for n in range(1, len(tiles)):
                code_row = jnp.where(group == n, codes[tiles[n]][:, :depth], code_row)
            matches = []
            for oz in (-1, 0, 1):
                for ox, oy in tiles:
                    wanted = own_code + float(ox * 1024 + oy * 32 + oz)
                    matches.append(jnp.where(wanted == code_row, 1.0, 0.0))
            picks[(ax, ay)] = (tiles, jnp.concatenate(matches, axis=0).astype(BF16))

    def padded(cell, shift):
        return 0 if shift < 0 else (5 if shift > 0 else cell + 1)

    def assemble(field, faces, diags):
        def source(dx, dy, i, j, k):
            if dx == 0 and dy == 0:
                return field[i + 1, j + 1, k + 1]
            is_face, slot = face_slot(-dx, -dy)
            if not is_face:
                return diags[slot, k]
            return faces[slot, (j if dy == 0 else i) * 4 + k]

        for (ax, ay), (tiles, pick) in picks.items():
            count = len(tiles)
            for i in {-1: (3,), 0: (1, 2), 1: (0,)}[ax]:
                for j in {-1: (3,), 0: (1, 2), 1: (0,)}[ay]:
                    for k in range(4):
                        shifts = {0: (0, 1), 3: (-1, 0)}.get(k, (0,))
                        if count == 1 and k in (1, 2):
                            continue
                        first = (shifts[0] + 1) * count * NB
                        last = (shifts[-1] + 2) * count * NB
                        pool = [source(dx, dy, i, j, k) for dx, dy in tiles]
                        pool = pool[0] if count == 1 else jnp.concatenate(pool, axis=0)
                        got = exact_dot(pick[first:last], pool).astype(BF16)
                        row = 0
                        for oz in shifts:
                            for ox, oy in tiles:
                                if ox or oy or oz:
                                    to = padded(i, ox), padded(j, oy), padded(k, oz)
                                    field[to] = got[row : row + NB]
                                row += NB

    assemble(field_u, halo_face, halo_diag)

    def window(field, tap):
        a, b, e = tap // 9, tap // 3 % 3, tap % 3
        return field[a : a + 4, b : b + 4, e : e + 4].reshape(1024, CH)

    kept_turned = field_g[1:5, 1:5, 1:5].reshape(1024, CH).T
    dw_full[TAPS * CH :] = jnp.zeros((dw_full.shape[0] - TAPS * CH, CH), F32)

    def gradient(first, last):
        for tap in range(first, last, 2):
            upto = min(tap + 2, last)
            right = [window(field_u, n) for n in range(tap, upto)]
            right = right[0] if len(right) == 1 else jnp.concatenate(right, axis=1)
            dw_full[tap * CH : upto * CH] = exact_dot(kept_turned, right).T

    def split(which):
        for n in range(plane):
            for part in range(2):
                start = (which * plane + n) * rows + part * half
                nx, ny = n % side, n // side
                to = (nx, ny) if part == 0 else (ny, nx)
                dw_parts[part, which, to[0], to[1]] = dw_full[start : start + half_pad]
        return push(
            dw_parts.at[1 - core, which],
            swap_in.at[which],
            r0_send.at[which],
            r0_recv.at[which],
            sibling,
        )

    def phase_one(which, swap):
        swap.wait()
        chip_sum[which] = dw_parts[core, which] + swap_in[which]
        copies = []
        for k, device in enumerate(peers1):
            index = which * (side - 1) + k
            copies.append(
                push(
                    chip_sum.at[which, ones[k]],
                    one_in.at[which, k],
                    r1_send.at[index],
                    r1_recv.at[index],
                    device,
                )
            )
        return copies

    def phase_two(which, arriving):
        for copy in arriving:
            copy.wait()
        total = chip_sum[which, pos1]
        for k in range(side - 1):
            total = total + one_in[which, k]
        one_sum[which] = total
        copies = []
        for k, device in enumerate(peers2):
            index = which * (side - 1) + k
            copies.append(
                push(
                    one_sum.at[which, twos[k]],
                    two_in.at[which, k],
                    r2_send.at[index],
                    r2_recv.at[index],
                    device,
                )
            )
        return copies

    def phase_done(which, arriving):
        for copy in arriving:
            copy.wait()
        total = one_sum[which, pos2]
        for k in range(side - 1):
            total = total + two_in[which, k]
        plane_sum[which] = total

    gradient(0, 14)
    swap_low = split(0)
    gradient(14, TAPS)
    swap_high = split(1)
    one_low = phase_one(0, swap_low)
    one_high = phase_one(1, swap_high)
    def convolve(field, weights, result_ref, i):
        total = None
        for tap in range(0, TAPS, 2):
            last = min(tap + 2, TAPS)
            left = []
            for n in range(tap, last):
                a, b, e = n // 9, n // 3 % 3, n % 3
                left.append(field[i + a, b : b + 4, e : e + 4].reshape(256, CH))
            left = left[0] if len(left) == 1 else jnp.concatenate(left, axis=1)
            term = exact_dot(left, weights[tap * CH : last * CH])
            total = term if total is None else total + term
        slab = exact_dot(turn_out, total.astype(BF16)).astype(BF16)
        result_ref[0, :, 16 * i : 16 * i + 16, :] = slab.reshape(NB, 16, CH)

    two_low = phase_two(0, one_low)
    two_high = phase_two(1, one_high)
    for copy in w_copies:
        copy.wait()
    ws_copy = push(w_parts.at[core], w_parts.at[core], ws_sem.at[0], ws_sem.at[1], sibling)
    ws_copy.wait()
    for which in range(2):
        for n in range(plane):
            nx, ny = n % side, n // side
            to = (nx, ny) if which == 0 else (ny, nx)
            start = (which * plane + n) * rows
            w_full[start : start + rows] = w_parts[which, to[0], to[1], 0:rows]
    for tap in range(TAPS):
        w_turned[(26 - tap) * CH : (27 - tap) * CH] = w_full[tap * CH : (tap + 1) * CH].T

    for i in range(0, 2):
        convolve(field_u, w_full, out_ref, i)
    phase_done(0, two_low)
    phase_done(1, two_high)

    def piece_start(low):
        start = low * piece
        return pl.multiple_of(jnp.minimum(start, half_pad - piece), 8)

    z_copies = []
    for k, device in enumerate(z_peers):
        low = lax.rem(zeds[k], z_low)
        z_copies.append(
            push(
                plane_sum.at[zeds[k] // z_low, pl.ds(piece_start(low), piece)],
                z_in.at[k],
                r3_send.at[k],
                r3_recv.at[k],
                device,
            )
        )
    for i in range(2, 4):
        convolve(field_u, w_full, out_ref, i)
    halo_wait(*g_refs)
    assemble(field_g, halo_gface, halo_gdiag)
    for copy in z_copies:
        copy.wait()
    total = plane_sum[zhi, pl.ds(piece_start(zlo), piece)]
    for k in range(z_all - 1):
        total = total + z_in[k]
    pieces[p] = total * (1.0 / math.sqrt(gx_size * gy_size * NB * 64))
    last_copies = []
    for k, device in enumerate(gx_peers):
        last_copies.append(push(pieces.at[p], pieces.at[p], r4_send.at[k], r4_recv.at[k], device))
    for i in range(0, 4):
        convolve(field_g, w_turned, gf_ref, i)
    for copy in last_copies:
        copy.wait()
    for n in range(gx_size):
        part, low = n % 2, n // 2
        start = min(low * piece, half_pad - piece)
        count = min(piece, half - start)
        gw_ref[part * half + start : part * half + start + count] = pieces[n, 0:count]


def deliver(a_ref, b_ref, c_ref, a_out, b_out, c_out):
    a_out[...] = a_ref[...]
    b_out[...] = b_ref[...]
    c_out[...] = c_ref[...]


def hand_over(*arrays):
    return pl.pallas_call(
        deliver,
        out_shape=tuple(jax.ShapeDtypeStruct(a.shape, a.dtype) for a in arrays),
        in_specs=[pl.BlockSpec(memory_space=pltpu.VMEM)] * 3,
        out_specs=[pl.BlockSpec(memory_space=pltpu.VMEM)] * 3,
    )(*arrays)


def local(gx_size, gy_size, features, block_at, block_coords, weight, cotangent):
    plane = gy_size // 2
    side = math.isqrt(plane)
    z_low = gx_size // 2
    z_all = 2 * z_low
    rows = TAPS * CH // gy_size
    rows_pad = -(-rows // 16) * 16
    half_pad = -(-(rows // 2) // 8) * 8
    piece = -(-half_pad // (8 * z_low)) * 8
    blocks = pl.BlockSpec(memory_space=pltpu.VMEM)
    vmem = pltpu.VMEM
    dma = pltpu.SemaphoreType.DMA
    corners = block_coords.transpose(1, 0, 2)
    positions = block_at.reshape(-1, block_at.shape[2])
    results = pl.pallas_call(
        functools.partial(kernel, gx_size, gy_size, side),
        out_shape=(
            jax.ShapeDtypeStruct(features.shape, BF16),
            jax.ShapeDtypeStruct(features.shape, BF16),
            jax.ShapeDtypeStruct((rows, CH), F32),
        ),
        in_specs=[pl.BlockSpec(memory_space=pl.ANY)] * 5,
        out_specs=[blocks] * 3,
        scratch_shapes=[
            vmem(features.shape, BF16),
            vmem(positions.shape, jnp.int32),
            vmem(corners.shape, jnp.int32),
            vmem(weight.shape, BF16),
            vmem(features.shape, BF16),
            vmem((6, 6, 6, NB, CH), BF16),
            vmem((6, 6, 6, NB, CH), BF16),
            vmem((4, 17, NB, CH), BF16),
            vmem((4, 5, NB, CH), BF16),
            vmem((4, 17, NB, CH), BF16),
            vmem((4, 5, NB, CH), BF16),
            vmem((4, 16, NB, CH), BF16),
            vmem((4, 4, NB, CH), BF16),
            vmem((4, 16, NB, CH), BF16),
            vmem((4, 4, NB, CH), BF16),
            vmem((2, rows_pad, CH), BF16),
            vmem((2, side, side, rows_pad, CH), BF16),
            vmem((TAPS * CH, CH), BF16),
            vmem((TAPS * CH, CH), BF16),
            vmem((TAPS * CH + 16, CH), F32),
            vmem((2, 2, side, side, half_pad, CH), F32),
            vmem((2, side, side, half_pad, CH), F32),
            vmem((2, side, side, half_pad, CH), F32),
            vmem((2, side - 1, side, half_pad, CH), F32),
            vmem((2, side, half_pad, CH), F32),
            vmem((2, side - 1, half_pad, CH), F32),
            vmem((2, half_pad, CH), F32),
            vmem((z_all - 1, piece, CH), F32),
            vmem((gx_size, piece, CH), F32),
            dma((5,)),
            dma((8,)),
            dma((8,)),
            dma((8,)),
            dma((8,)),
            dma((2,)),
            dma((plane - 1,)),
            dma((plane - 1,)),
            dma((2,)),
            dma((2,)),
            dma((2,)),
            dma((2 * side - 2,)),
            dma((2 * side - 2,)),
            dma((2 * side - 2,)),
            dma((2 * side - 2,)),
            dma((z_all - 1,)),
            dma((z_all - 1,)),
            dma((gx_size - 1,)),
            dma((gx_size - 1,)),
        ],
        compiler_params=pltpu.CompilerParams(
            collective_id=0, has_side_effects=True, vmem_limit_bytes=63 * 1024 * 1024
        ),
    )(features, positions, corners, weight, cotangent)
    return hand_over(*results)


def solution(mesh):
    placed = (
        P("gx", "gy", None, None),
        P("gx", "gy", None),
        P("gx", None, "gy"),
        P("gy", None),
        P("gx", "gy", None, None),
    )
    return jax.shard_map(
        functools.partial(local, mesh.shape["gx"], mesh.shape["gy"]),
        mesh=mesh,
        in_specs=placed,
        out_specs=(P("gx", "gy", None, None), P("gx", "gy", None, None), P("gy", None)),
        check_vma=False,
    )
```
